256 devices in a mesh: dp: 16 (over x, y_lo, core), shard: 16 (over z, y_hi).
Axes of the slice: x: 4, y: 4 (y_hi: 2, y_lo: 2; y = y_hi * 2 + y_lo), z: 8, core: 2. Of those that a mesh axis runs over, the one named last changes fastest.
Arguments:
- hidden: bfloat16 [2048, 16384], P('dp', 'shard'), may hold values from -6 to 6
- head_weight: bfloat16 [16384, 16384], P('shard', 'dp'), may hold values from -0.046875 to 0.046875
- vocab_head: bfloat16 [16384, 4096], P('shard'), may hold values from -0.0546875 to 0.0546875
- targets: int32 [2048], P('dp'), may hold values from 0 to 4095
Outputs:
- grad_weight: bfloat16 [16384, 16384], P('dp', 'shard')
- token_loss: float32 [2048], P('dp')
The draws below stay inside these ranges and needn't reach their ends.
All inputs are finite; a program needn't handle non-finite values.
Results may differ from the reference program's by a relative error of at most 0.014.
Values may be sent and summed in bfloat16 or wider, within the bound.
A program may use at most 128 MiB of HBM per device.

```python
import math
import jax
import jax.numpy as jnp
import numpy as np
from jax import lax

D = 16384
TOKENS = 2048
VOC = 4096


def draw_hidden(key, part):
    key = jax.random.fold_in(key, 11)
    key_common, key_private = jax.random.split(key, 2)
    groups = TOKENS // 128
    common = jax.random.normal(key_common, (groups, D), jnp.float32)
    scales = jnp.full((groups, 1), 0.9, jnp.float32)
    private = 0.45 * jax.random.normal(key_private, (TOKENS, D), jnp.float32)
    shared = jnp.repeat(common * scales, 128, axis=0)
    return jnp.clip(shared + private, -6.0, 6.0).astype(jnp.bfloat16)


def touch_ends(drawn, own_key, low, largest):
    longest = drawn.shape.index(max(drawn.shape))
    spots = []
    for shift in (0, 1):
        where = [jax.random.randint(jax.random.fold_in(own_key, axis), (), 0, length) for axis, length in enumerate(drawn.shape)]
        where[longest] = (where[longest] + shift) % drawn.shape[longest]
        spots.append(tuple(where))
    return drawn.at[spots[0]].set(low).at[spots[1]].set(largest)


def levels(key, shape, cuts, low, high):
    level = 1.0
    for axis_at, parts in cuts:
        draws = jax.random.uniform(jax.random.fold_in(jax.random.fold_in(key, 6), axis_at), (parts,), jnp.float32, low / len(cuts), high / len(cuts))
        level = level * jnp.repeat(jnp.exp(draws), shape[axis_at] // parts).reshape((-1,) + (1,) * (len(shape) - 1 - axis_at))
    return level


def rank_table(number_of, lean):
    portions = [(1 << 20) // math.isqrt(standing ** lean) + 1 for standing in range(1, number_of + 1)]
    deviation = 1 + sum(portions) // (1 << 30)
    return np.cumsum(np.array([max(1, weight // deviation) for weight in portions]))


def ranked_ids(own_key, shape, number_of, slope):
    grid = rank_table(number_of, slope)
    lot = jax.random.randint(jax.random.fold_in(own_key, 1), shape, 0, int(grid[number_of - 1]))
    grade = jnp.searchsorted(jnp.asarray(grid, jnp.int32), lot, side="right")
    return jax.random.permutation(jax.random.fold_in(own_key, 2), number_of)[grade].astype(jnp.int32)


def scatter_about(key, dims, width, limit, pieces=(), dtype=jnp.bfloat16):
    drawn = jax.random.normal(key, dims, jnp.float32) * width
    if len(pieces) > 0:
        drawn = levels(key, dims, pieces, -0.22, 0.18) * drawn
    return jnp.clip(drawn, min=-limit, max=limit).astype(dtype)


def setup_inputs(seed: int = 0) -> dict:
    key_list = jax.random.split(jax.random.key(seed), 5)
    hidden = draw_hidden(jax.random.fold_in(key_list[4], 71), 0)
    head_weight = scatter_about(key_list[1], (D, D), D ** -0.5, 0.046875, ((0, 16), (1, 16)))
    vocab_head = scatter_about(key_list[2], (D, VOC), (2 * D // 3) ** -0.5, 0.0546875, ((0, 16),))
    targets = touch_ends(ranked_ids(key_list[3], (TOKENS,), VOC, 2), jax.random.fold_in(key_list[3], 3), 0, VOC - 1).astype(jnp.int32)
    return dict(hidden=hidden, head_weight=head_weight, vocab_head=vocab_head, targets=targets)


def reference(hidden, head_weight, vocab_head, targets):
    pre = jnp.dot(hidden, head_weight, preferred_element_type=jnp.float32)
    resout = (hidden.astype(jnp.float32) + jax.nn.silu(pre)).astype(jnp.bfloat16)
    logits = jnp.dot(resout, vocab_head, preferred_element_type=jnp.float32)
    expo = jnp.exp(logits)
    total = jnp.sum(expo, axis=1)
    positions = lax.broadcasted_iota(jnp.int32, (TOKENS, VOC), 1)
    onehot = (positions == targets.astype(jnp.int32)[:, None]).astype(jnp.float32)
    picked = jnp.sum(onehot * logits, axis=1)
    token_loss = jnp.log(total) - picked
    grads = (expo / total[:, None] - onehot).astype(jnp.bfloat16)
    dres = jnp.dot(grads, vocab_head.T, preferred_element_type=jnp.float32)
    sig = jax.nn.sigmoid(pre)
    dpre = (dres * (sig * (1.0 + pre * (1.0 - sig)))).astype(jnp.bfloat16)
    blocks = dpre.T.reshape(16, D // 16, TOKENS)

    def one_block(block_rows):
        return jnp.dot(block_rows, hidden, preferred_element_type=jnp.float32).astype(jnp.bfloat16)

    grad_weight = lax.map(one_block, blocks).reshape(D, D)
    return grad_weight, token_loss
```

```python
import jax
import jax.numpy as jnp
from jax import lax
from jax.experimental import pallas as pl
from jax.experimental.pallas import tpu as pltpu
from jax.sharding import PartitionSpec as P

MESH = pl.DeviceIdType.MESH
BF16 = jnp.bfloat16
F32 = jnp.float32

ROUNDS = 8
RING = 8
PARTS = 4


def slot_of(dx, a):
    odd = dx % 2
    return odd * (2 + 2 * a + (3 - dx) // 2) + (1 - odd) * (3 * dx + a)


def offset_of(slot):
    middle = jnp.logical_and(slot >= 2, slot <= 5)
    dx = jnp.where(middle, 3 - 2 * (slot % 2), jnp.where(slot >= 6, 2, 0))
    a = jnp.where(middle, (slot // 2 + 1) % 2, slot % 2)
    return dx, a


def send(src, dst, send_sem, recv_sem, device):
    pltpu.make_async_remote_copy(
        src_ref=src,
        dst_ref=dst,
        send_sem=send_sem,
        recv_sem=recv_sem,
        device_id=device,
        device_id_type=MESH,
    ).start()


def wait(ref, sem):
    pltpu.make_async_copy(ref, ref, sem).wait()


def kernel(
    h_in, w_in, v_in, tgt, out, loss_out,
    H, W, V, PT, S0, R, YS, YK, YR, TS, PRE, RES, D1, L, SL, RL, LYS, LYR, LF, G, DR, DQ, DP, ACC, OUT,
    loc, h_sib, h_far, h_r, rs_s, rs_r, y_s, y_r, t_s, t_r, l_s, l_r, ly_s, ly_r, g_s, g_r,
    d_s, d_r, dy_s, dy_r, a_s, a_r, o_s,
):
    dp = lax.axis_index("dp")
    shard = lax.axis_index("shard")
    x, y_lo, core = dp // 4, (dp // 2) % 2, dp % 2
    z, y_hi = shard // 2, shard % 2
    feats = H.shape[3]
    units = W.shape[1]
    vq = L.shape[3]
    voc = vq * PARTS

    x_next = ((dp + 4) % 16, shard)
    x_prev = ((dp + 12) % 16, shard)
    y_near = (dp + 2 - 4 * y_lo, shard)
    sibling = (dp + 1 - 2 * core, shard)
    z_next = (dp, (shard + 2) % 16)
    z_prev = (dp, (shard + 14) % 16)
    y_far = (dp, shard + 1 - 2 * y_hi)
    ring = (z_next, z_prev)

    def out_target(slot):
        dx, a = offset_of(slot)
        there = ((x + dx) % 4) * 4 + ((y_lo + a) % 2) * 2 + (core + shard // 8) % 2
        return (there, dp)

    flip = (core + shard % 2) % 2

    def in_source(g):
        return (shard, 8 * flip + g)

    def is_self(device):
        return jnp.logical_and(device[0] == dp, device[1] == shard)

    barrier = pltpu.get_barrier_semaphore()
    for device in (x_next, x_prev, y_near, sibling, z_next, z_prev, y_far):
        pl.semaphore_signal(barrier, inc=1, device_id=device, device_id_type=MESH)
    for n in range(8):
        for device in (out_target(jnp.int32(n)), in_source(n)):
            @pl.when(jnp.logical_not(is_self(device)))
            def _(device=device):
                pl.semaphore_signal(barrier, inc=1, device_id=device, device_id_type=MESH)
    own = jnp.logical_and(dp == shard, dp < 8)
    copy_w = pltpu.make_async_copy(w_in, W, loc.at[0])
    copy_w.start()
    copy_v = pltpu.make_async_copy(v_in, V, loc.at[1])
    copy_h = pltpu.make_async_copy(h_in, H.at[0, 0], loc.at[2])
    copy_h.start()
    pl.semaphore_wait(barrier, jnp.where(own, 21, 23))

    send(h_in, H.at[0, 1], h_sib.at[0], h_r.at[0, 1], sibling)
    send(h_in, H.at[1, 0], h_far.at[0], h_r.at[1, 0], y_near)
    send(h_in, H.at[2, 0], h_far.at[1], h_r.at[2, 0], x_next)
    send(h_in, H.at[3, 0], h_far.at[2], h_r.at[3, 0], x_prev)
    copy_v.start()

    def service(q):
        wait(H.at[q, 0], h_r.at[q, 0])
        send(H.at[q, 0], H.at[q, 1], h_sib.at[q], h_r.at[q, 1], sibling)

        @pl.when(q == 1)
        def _():
            send(H.at[1, 0], H.at[4, 0], h_far.at[3], h_r.at[4, 0], x_next)
            send(H.at[1, 0], H.at[5, 0], h_far.at[4], h_r.at[5, 0], x_prev)

        @pl.when(q == 2)
        def _():
            send(H.at[2, 0], H.at[6, 0], h_far.at[5], h_r.at[6, 0], x_next)

        @pl.when(q == 5)
        def _():
            send(H.at[5, 0], H.at[7, 0], h_far.at[6], h_r.at[7, 0], x_prev)

    copy_h.wait()
    copy_w.wait()

    def ahead(d, k):
        return (z + (RING // 2 - k if d == 0 else RING // 2 + k)) % RING

    nt = min(512, units)

    def product(t):
        def tile(n, _):
            cols = pl.ds(pl.multiple_of(n * nt, nt), nt)
            rows = H[t].reshape(256, feats)
            PT[t, :, :, cols] = jnp.dot(
                rows, W[:, cols], preferred_element_type=F32
            ).reshape(RING, 32, nt)
            return 0

        lax.fori_loop(0, units // nt, tile, 0)

    def live(r, n):
        return jnp.logical_and(r >= 0, r < n)

    def pre_tick(t, _):
        r5 = t - 5

        @pl.when(live(r5, ROUNDS))
        def _():
            wait(YR.at[r5], y_r.at[r5])
            TS[r5] = (YK[r5] + YR[r5].astype(F32)).astype(BF16)
            device = out_target(r5)
            g = shard % 8

            @pl.when(is_self(device))
            def _():
                pltpu.make_async_copy(TS.at[r5], PRE.at[g], t_r.at[g]).start()

            @pl.when(jnp.logical_not(is_self(device)))
            def _():
                send(TS.at[r5], PRE.at[g], t_s.at[r5], t_r.at[g], device)

        r4 = t - 4

        @pl.when(live(r4, ROUNDS))
        def _():
            wait(R.at[0, r4, 3], rs_r.at[0, r4, 3])
            wait(R.at[1, r4, 3], rs_r.at[1, r4, 3])
            mine = pl.ds(pl.multiple_of(y_hi * 16, 16), 16)
            other = pl.ds(pl.multiple_of(16 - y_hi * 16, 16), 16)
            YS[r4] = (
                PT[r4, z, other] + R[0, r4, 3, other].astype(F32) + R[1, r4, 3, other].astype(F32)
            ).astype(BF16)
            send(YS.at[r4], YR.at[r4], y_s.at[r4], y_r.at[r4], y_far)
            YK[r4] = PT[r4, z, mine] + R[0, r4, 3, mine].astype(F32) + R[1, r4, 3, mine].astype(F32)

        for k in (3, 2, 1):
            rk = t - k

            @pl.when(live(rk, ROUNDS))
            def _(k=k, rk=rk):
                for d in (0, 1):
                    at = ahead(d, k)
                    if k == 1:
                        half = slice(d * 16, d * 16 + 16)
                        rest = slice(16 - d * 16, 32 - d * 16)
                        wait(R.at[d, rk, 0, half], rs_r.at[d, rk, 0])
                        R[d, rk, 0, half] = (
                            PT[rk, at, half] + R[d, rk, 0, half].astype(F32)
                        ).astype(BF16)
                        R[d, rk, 0, rest] = PT[rk, at, rest].astype(BF16)
                    else:
                        wait(R.at[d, rk, k - 1], rs_r.at[d, rk, k - 1])
                        R[d, rk, k - 1] = (
                            PT[rk, at] + R[d, rk, k - 1].astype(F32)
                        ).astype(BF16)
                    send(R.at[d, rk, k - 1], R.at[d, rk, k], rs_s.at[d, rk, k], rs_r.at[d, rk, k], ring[d])

        @pl.when(t == 1)
        def _():
            service(t)

        @pl.when(t < ROUNDS)
        def _():
            wait(H.at[t, 1], h_r.at[t, 1])
            product(t)
            for d in (0, 1):
                half = slice(d * 16, d * 16 + 16)
                S0[d, t] = PT[t, ahead(d, 0), half].astype(BF16)
                send(S0.at[d, t], R.at[d, t, 0, half], rs_s.at[d, t, 0], rs_r.at[d, t, 0], ring[d])

        @pl.when(jnp.logical_and(t >= 1, t < ROUNDS - 1))
        def _():
            service(t + 1)

        return 0

    lax.fori_loop(0, ROUNDS + 5, pre_tick, 0)

    for g in range(8):
        wait(PRE.at[g], t_r.at[g])
    pre = PRE[...].reshape(128, units).astype(F32)
    RES[...] = (H[0, 0].astype(F32) + pre / (1.0 + jnp.exp(-pre))).astype(BF16)
    copy_v.wait()

    hc = vq // 2

    def logit_tick(t, _):
        p5 = t - 5

        @pl.when(live(p5, PARTS))
        def _():
            wait(LYR.at[p5], ly_r.at[p5])
            LF[p5] = LYS[p5].astype(F32) + LYR[p5].astype(F32)

        p4 = t - 4

        @pl.when(live(p4, PARTS))
        def _():
            wait(RL.at[0, p4, 3], l_r.at[0, p4, 3])
            wait(RL.at[1, p4, 3], l_r.at[1, p4, 3])
            LYS[p4] = (
                L[p4, z] + RL[0, p4, 3].astype(F32) + RL[1, p4, 3].astype(F32)
            ).astype(BF16)
            send(LYS.at[p4], LYR.at[p4], ly_s.at[p4], ly_r.at[p4], y_far)

        for k in (3, 2, 1):
            pk = t - k

            @pl.when(live(pk, PARTS))
            def _(k=k, pk=pk):
                for d in (0, 1):
                    at = ahead(d, k)
                    if k == 1:
                        half = slice(d * hc, d * hc + hc)
                        rest = slice(hc - d * hc, 2 * hc - d * hc)
                        wait(RL.at[d, pk, 0, :, half], l_r.at[d, pk, 0])
                        RL[d, pk, 0, :, half] = (
                            L[pk, at, :, half] + RL[d, pk, 0, :, half].astype(F32)
                        ).astype(BF16)
                        RL[d, pk, 0, :, rest] = L[pk, at, :, rest].astype(BF16)
                    else:
                        wait(RL.at[d, pk, k - 1], l_r.at[d, pk, k - 1])
                        RL[d, pk, k - 1] = (
                            L[pk, at] + RL[d, pk, k - 1].astype(F32)
                        ).astype(BF16)
                    send(RL.at[d, pk, k - 1], RL.at[d, pk, k], l_s.at[d, pk, k], l_r.at[d, pk, k], ring[d])

        @pl.when(t < PARTS)
        def _():
            cols = pl.ds(pl.multiple_of(t * vq, vq), vq)
            L[t] = jnp.dot(RES[...], V[:, cols], preferred_element_type=F32).reshape(RING, 16, vq)
            for d in (0, 1):
                half = slice(d * hc, d * hc + hc)
                SL[d, t] = L[t, ahead(d, 0), :, half].astype(BF16)
                send(SL.at[d, t], RL.at[d, t, 0, :, half], l_s.at[d, t, 0], l_r.at[d, t, 0], ring[d])

        return 0

    lax.fori_loop(0, PARTS + 5, logit_tick, 0)

    total = jnp.zeros((16, 1), F32)
    picked = jnp.zeros((16, 1), F32)
    target = tgt[z]
    for p in range(PARTS):
        logits = LF[p]
        hit = lax.broadcasted_iota(jnp.int32, (16, vq), 1) + p * vq == target
        total += jnp.sum(jnp.exp(logits), axis=1, keepdims=True)
        picked += jnp.sum(jnp.where(hit, logits, 0.0), axis=1, keepdims=True)
    for p in range(PARTS):
        hit = lax.broadcasted_iota(jnp.int32, (16, vq), 1) + p * vq == target
        G[z, :, p * vq:(p + 1) * vq] = (
            jnp.exp(LF[p]) / total - jnp.where(hit, 1.0, 0.0)
        ).astype(BF16)
    loss = jnp.log(total) - picked
    high = loss.astype(BF16).astype(F32)
    middle = (loss - high).astype(BF16).astype(F32)
    low = loss - high - middle
    lane = lax.broadcasted_iota(jnp.int32, (16, 128), 1)
    G[z, :, voc:] = jnp.where(
        lane == 0, high, jnp.where(lane == 1, middle, jnp.where(lane == 2, low, 0.0))
    ).astype(BF16)

    spans = ((0, voc // 4, voc // 2), (voc // 2, 3 * voc // 4, voc + 128))

    def behind(d, k):
        return (z + (RING - k if d == 0 else k)) % RING

    def span(p, d):
        return slice(spans[p][d], spans[p][d + 1])

    def grad_step(p, k):
        for d in (0, 1):
            every = slice(spans[p][0], spans[p][2])
            here = behind(d, k)
            if k > 0:
                got = span(p, d) if k == 4 else every
                wait(G.at[here, :, got], g_r.at[d, p, k - 1])
            if k < 4:
                some = span(p, d) if k == 3 else every
                piece = G.at[here, :, some]
                send(piece, piece, g_s.at[d, p, k], g_r.at[d, p, k], ring[d])

    def gradient(p):
        cols = slice(p * voc // 2, (p + 1) * voc // 2)
        return lax.dot_general(
            G[:, :, cols].reshape(128, voc // 2), V[:, cols], (((1,), (1,)), ((), ())),
            preferred_element_type=F32,
        )

    for t in range(6):
        for k in (4, 3, 2, 1, 0):
            if 0 <= t - k < 2:
                grad_step(t - k, k)
        if t == 1:
            again = PRE[...].reshape(128, units).astype(F32)
            sig = 1.0 / (1.0 + jnp.exp(-again))
            D1[...] = sig * (1.0 + again * (1.0 - sig))
            ACC[...] = jnp.zeros_like(ACC)
        if t == 4:
            DR[...] = gradient(0)
    DQ[...] = ((DR[...] + gradient(1)) * D1[...]).astype(BF16).reshape(8, 16, units)

    slot = slot_of((x + 4 - shard // 4) % 4, (y_lo + (shard // 2) % 2) % 2)
    for g in range(8):
        device = in_source(g)
        place = DP.at[slot, 4 * flip + g // 2, g % 2 * 16:g % 2 * 16 + 16]

        @pl.when(is_self(device))
        def _(g=g, place=place):
            pltpu.make_async_copy(DQ.at[g], place, d_r.at[slot]).start()

        @pl.when(jnp.logical_not(is_self(device)))
        def _(g=g, place=place, device=device):
            send(DQ.at[g], place, d_s.at[g], d_r.at[slot], device)

    loss_out[...] = jnp.broadcast_to(
        jnp.sum(G[:, :, voc:].astype(F32), axis=2, keepdims=True), loss_out.shape
    )

    mt = min(256, units)

    def weight_tick(t, _):
        for k in (5, 4, 3, 2):
            rk = t - k

            @pl.when(live(rk, ROUNDS))
            def _(k=k, rk=rk):
                for d in (0, 1):
                    here = behind(d, k - 1)
                    half = slice(d * 16, d * 16 + 16)
                    if k == 5:
                        wait(DP.at[rk, here, half], a_r.at[d, rk, 3])
                        continue
                    wait(DP.at[rk, here], a_r.at[d, rk, k - 2])
                    piece = DP.at[rk, here, half] if k == 4 else DP.at[rk, here]
                    send(piece, piece, a_s.at[d, rk, k - 1], a_r.at[d, rk, k - 1], ring[d])

        r1 = t - 1

        @pl.when(live(r1, ROUNDS))
        def _():
            other = pl.ds(pl.multiple_of(16 - y_hi * 16, 16), 16)
            wait(DP.at[r1, z, other], dy_r.at[r1])
            piece = DP.at[r1, z]
            for d in (0, 1):
                send(piece, piece, a_s.at[d, r1, 0], a_r.at[d, r1, 0], ring[d])

        @pl.when(t < ROUNDS)
        def _():
            mine = pl.ds(pl.multiple_of(y_hi * 16, 16), 16)
            piece = DP.at[t, z, mine]
            wait(piece, d_r.at[t])
            send(piece, piece, dy_s.at[t], dy_r.at[t], y_far)

        r5 = t - 5

        @pl.when(live(r5, ROUNDS))
        def _():
            def tile(m, _):
                cols = pl.ds(pl.multiple_of(m * mt, mt), mt)
                ACC[cols, :] += lax.dot_general(
                    DP[r5, :, :, cols].reshape(256, mt), H[r5].reshape(256, feats),
                    (((0,), (0,)), ((), ())), preferred_element_type=F32,
                )
                return 0

            lax.fori_loop(0, units // mt, tile, 0)

        return 0

    lax.fori_loop(0, ROUNDS + 5, weight_tick, 0)

    def finish(m, _):
        rows = pl.ds(pl.multiple_of(m * mt, mt), mt)
        OUT[rows, :] = ACC[rows, :].astype(BF16)
        pltpu.make_async_copy(OUT.at[rows], out.at[rows], o_s.at[m]).start()
        return 0

    lax.fori_loop(0, units // mt, finish, 0)

    for n in range(7):
        wait(H.at[0, 0], h_far.at[n])

    def sent(r, _):
        wait(H.at[0, 0], h_sib.at[r])
        wait(YS.at[r], y_s.at[r])
        wait(DP.at[r, 0, 0:16], dy_s.at[r])

        @pl.when(jnp.logical_not(is_self(out_target(r))))
        def _():
            wait(TS.at[r], t_s.at[r])

        @pl.when(jnp.logical_not(is_self(in_source(r))))
        def _():
            wait(DQ.at[r], d_s.at[r])

        for d in (0, 1):
            wait(S0.at[d, r], rs_s.at[d, r, 0])
            wait(DP.at[r, 0, 0:16], a_s.at[d, r, 3])
            for k in range(3):
                wait(R.at[d, r, 0], rs_s.at[d, r, k + 1])
                wait(DP.at[r, 0], a_s.at[d, r, k])
        return 0

    lax.fori_loop(0, ROUNDS, sent, 0)

    def sent_logits(p, _):
        wait(LYS.at[p], ly_s.at[p])
        for d in (0, 1):
            wait(SL.at[d, p], l_s.at[d, p, 0])
            for k in range(3):
                wait(RL.at[d, p, 0], l_s.at[d, p, k + 1])
        return 0

    lax.fori_loop(0, PARTS, sent_logits, 0)
    for p in range(2):
        for d in (0, 1):
            for k in range(4):
                some = span(p, d) if k == 3 else slice(spans[p][0], spans[p][2])
                wait(G.at[0, :, some], g_s.at[d, p, k])
    for m in range(units // mt):
        rows = slice(m * mt, (m + 1) * mt)
        pltpu.make_async_copy(OUT.at[rows], out.at[rows], o_s.at[m]).wait()


def body(hidden, head_weight, vocab_head, targets):
    feats, units = head_weight.shape
    voc = vocab_head.shape[1]
    vq = voc // PARTS
    dma = pltpu.SemaphoreType.DMA
    vmem = pltpu.VMEM
    scratch = [
        vmem((ROUNDS, 2, 128, feats), BF16),
        vmem((feats, units), BF16),
        vmem((units, voc), BF16),
        vmem((ROUNDS, RING, 32, units), F32),
        vmem((2, ROUNDS, 16, units), BF16),
        vmem((2, ROUNDS, 4, 32, units), BF16),
        vmem((ROUNDS, 16, units), BF16),
        vmem((ROUNDS, 16, units), F32),
        vmem((ROUNDS, 16, units), BF16),
        vmem((ROUNDS, 16, units), BF16),
        vmem((8, 16, units), BF16),
        vmem((128, units), BF16),
        vmem((128, units), F32),
        vmem((PARTS, RING, 16, vq), F32),
        vmem((2, PARTS, 16, vq // 2), BF16),
        vmem((2, PARTS, 4, 16, vq), BF16),
        vmem((PARTS, 16, vq), BF16),
        vmem((PARTS, 16, vq), BF16),
        vmem((PARTS, 16, vq), F32),
        vmem((RING, 16, voc + 128), BF16),
        vmem((128, units), F32),
        vmem((8, 16, units), BF16),
        vmem((ROUNDS, RING, 32, units), BF16),
        vmem((units, feats), F32),
        vmem((units, feats), BF16),
        dma((3,)),
        dma((8,)), dma((7,)), dma((8, 2)),
        dma((2, ROUNDS, 4)), dma((2, ROUNDS, 4)),
        dma((ROUNDS,)), dma((ROUNDS,)),
        dma((ROUNDS,)), dma((8,)),
        dma((2, PARTS, 4)), dma((2, PARTS, 4)),
        dma((PARTS,)), dma((PARTS,)),
        dma((2, 2, 4)), dma((2, 2, 4)),
        dma((8,)), dma((ROUNDS,)),
        dma((ROUNDS,)), dma((ROUNDS,)),
        dma((2, ROUNDS, 4)), dma((2, ROUNDS, 4)),
        dma((max(1, units // 256),)),
    ]
    anywhere = pl.BlockSpec(memory_space=pl.ANY)
    inside = pl.BlockSpec(memory_space=pltpu.VMEM)
    grad, loss = pl.pallas_call(
        kernel,
        out_shape=[
            jax.ShapeDtypeStruct((units, feats), BF16),
            jax.ShapeDtypeStruct((RING, 16, 128), F32),
        ],
        in_specs=[anywhere, anywhere, anywhere, inside],
        out_specs=[anywhere, inside],
        scratch_shapes=scratch,
        compiler_params=pltpu.CompilerParams(
            collective_id=0, has_side_effects=True, vmem_limit_bytes=56 * 1024 * 1024
        ),
        name="head",
    )(hidden, head_weight, vocab_head, targets.reshape(RING, 16, 1))
    return grad, loss[:, :, 0].reshape(targets.shape)


def solution(mesh):
    in_specs = (P("dp", "shard"), P("shard", "dp"), P("shard", None), P("dp"))
    out_specs = (P("dp", "shard"), P("dp"))
    return jax.shard_map(body, mesh=mesh, in_specs=in_specs, out_specs=out_specs, check_vma=False)
```

```python
import jax
import jax.numpy as jnp
from jax import lax
from jax.experimental import pallas as pl
from jax.experimental.pallas import tpu as pltpu
from jax.sharding import PartitionSpec as P

MESH = pl.DeviceIdType.MESH
BF16 = jnp.bfloat16
F32 = jnp.float32

ROUNDS = 8
RING = 8
PARTS = 4


def slot_of(dx, a):
    odd = dx % 2
    return odd * (2 + 2 * a + (3 - dx) // 2) + (1 - odd) * (3 * dx + a)


def offset_of(slot):
    middle = jnp.logical_and(slot >= 2, slot <= 5)
    dx = jnp.where(middle, 3 - 2 * (slot % 2), jnp.where(slot >= 6, 2, 0))
    a = jnp.where(middle, (slot // 2 + 1) % 2, slot % 2)
    return dx, a


def send(src, dst, send_sem, recv_sem, device):
    pltpu.make_async_remote_copy(
        src_ref=src,
        dst_ref=dst,
        send_sem=send_sem,
        recv_sem=recv_sem,
        device_id=device,
        device_id_type=MESH,
    ).start()


def wait(ref, sem):
    pltpu.make_async_copy(ref, ref, sem).wait()


def kernel(
    h_in, w_in, v_in, tgt, out, loss_out,
    H, W, V, PT, S0, R, YS, YK, YR, YB, YC, TS, PRE, RES, D1, L, SL, RL, LYS, LYR, LF, G, LT, DR, DQ, DP,
    ACC, OUT,
    loc, h_s, h_r, rs_s, rs_r, y_s, y_r, yc_r, t_s, t_r, l_s, l_r, ly_s, ly_r, g_s, g_r, lt_s, lt_r,
    d_s, d_r, dy_s, dy_r, a_s, a_r, o_s,
):
    dp = lax.axis_index("dp")
    shard = lax.axis_index("shard")
    x, y_lo, core = dp // 4, (dp // 2) % 2, dp % 2
    z, y_hi = shard // 2, shard % 2
    y_other = 1 - y_hi
    feats = H.shape[2]
    units = W.shape[1]
    vq = L.shape[3]
    hu, hc = units // 2, vq // 2

    x_next = ((dp + 4) % 16, shard)
    x_prev = ((dp + 12) % 16, shard)
    y_near = (dp + 2 - 4 * y_lo, shard)
    sibling = (dp + 1 - 2 * core, shard)
    z_next = (dp, (shard + 2) % 16)
    z_prev = (dp, (shard + 14) % 16)
    y_far = (dp, shard + 1 - 2 * y_hi)
    ring = (z_next, z_prev)

    def out_target(slot):
        dx, a = offset_of(slot)
        there = ((x + dx) % 4) * 4 + ((y_lo + a) % 2) * 2 + (core + y_hi) % 2
        return (there, dp)

    flip = (core + shard % 2) % 2

    def in_source(g):
        return (shard, 2 * g + flip)

    def is_self(device):
        return jnp.logical_and(device[0] == dp, device[1] == shard)

    own = jnp.logical_and(dp == shard, y_hi == 0)

    barrier = pltpu.get_barrier_semaphore()
    near = (x_next, x_prev, y_near, sibling, z_next, z_prev, y_far)
    for device in near:
        pl.semaphore_signal(barrier, inc=1, device_id=device, device_id_type=MESH)
    copy_w = pltpu.make_async_copy(w_in, W, loc.at[0])
    copy_w.start()
    copy_h = pltpu.make_async_copy(h_in, H.at[0], loc.at[2])
    copy_h.start()
    copy_v = pltpu.make_async_copy(v_in, V, loc.at[1])
    pl.semaphore_wait(barrier, len(near))

    def pass_on(src, slot, device):
        send(src, H.at[slot], h_s, h_r.at[slot], device)

    pass_on(h_in, 1, sibling)
    pass_on(h_in, 2, y_near)
    pass_on(h_in, 4, x_next)
    pass_on(h_in, 6, x_prev)
    copy_v.start()

    def service(q):
        wait(H.at[2 * q], h_r.at[2 * q])
        pass_on(H.at[2 * q], 2 * q + 1, sibling)

        @pl.when(q == 1)
        def _():
            pass_on(H.at[2], 8, x_next)
            pass_on(H.at[2], 10, x_prev)

        @pl.when(q == 2)
        def _():
            pass_on(H.at[4], 12, x_next)

        @pl.when(q == 5)
        def _():
            pass_on(H.at[10], 14, x_prev)

    copy_h.wait()
    copy_w.wait()

    def ahead(d, k):
        return (z + (RING // 2 - k if d == 0 else RING // 2 + k)) % RING

    def behind(d, k):
        return (z + (RING - k if d == 0 else k)) % RING

    def live(r, n):
        return jnp.logical_and(r >= 0, r < n)

    nt = min(512, units)

    def product(t):
        def tile(n, _):
            cols = pl.ds(pl.multiple_of(n * nt, nt), nt)
            rows = H[pl.ds(2 * t, 2)].reshape(256, feats)
            PT[t, :, :, :, cols] = jnp.dot(
                rows, W[:, cols], preferred_element_type=F32
            ).reshape(2, RING, 16, nt)
            return 0

        lax.fori_loop(0, units // nt, tile, 0)

    def even_step(r, s):
        q = r // 2
        if s == 0:
            for d in (0, 1):
                S0[d, r] = PT[r, d, ahead(d, 0)].astype(BF16)
                send(S0.at[d, r], R.at[d, r, 0, d], rs_s.at[0], rs_r.at[d, r, 0], ring[d])
        elif s < 4:
            for d in (0, 1):
                at = ahead(d, s)
                if s == 1:
                    wait(R.at[d, r, 0, d], rs_r.at[d, r, 0])
                    R[d, r, 0, d] = (PT[r, d, at] + R[d, r, 0, d].astype(F32)).astype(BF16)
                    R[d, r, 0, 1 - d] = PT[r, 1 - d, at].astype(BF16)
                else:
                    wait(R.at[d, r, s - 1], rs_r.at[d, r, s - 1])
                    R[d, r, s - 1] = (PT[r, :, at] + R[d, r, s - 1].astype(F32)).astype(BF16)
                send(R.at[d, r, s - 1], R.at[d, r, s], rs_s.at[1], rs_r.at[d, r, s], ring[d])
        elif s == 4:
            wait(R.at[0, r, 3], rs_r.at[0, r, 3])
            wait(R.at[1, r, 3], rs_r.at[1, r, 3])

            def total(h):
                return PT[r, h, z] + R[0, r, 3, h].astype(F32) + R[1, r, 3, h].astype(F32)

            YS[q] = total(y_other).astype(BF16)
            send(YS.at[q], YR.at[q], y_s.at[0], y_r.at[q], y_far)
            YK[q] = total(y_hi)
        else:
            wait(YR.at[q], y_r.at[q])
            TS[r] = (YK[q] + YR[q].astype(F32)).astype(BF16)

    groups = ((0, 1), (1, 3), (3, 5), (5, 7), (7, 8))

    def odd_step(r, s):
        q = r // 2
        if s == 0:
            for n, (low, high) in enumerate(groups):
                YB[q, low] = PT[r, y_other, ahead(0, n)].astype(BF16)
                if high - low == 2:
                    YB[q, low + 1] = PT[r, y_other, ahead(1, n)].astype(BF16)
                send(YB.at[q, low:high], YC.at[q, low:high], y_s.at[1], yc_r.at[q, n], y_far)
            return
        k = s - 1
        low, high = groups[k]
        wait(YC.at[q, low:high], yc_r.at[q, k])

        def mine(d, cols=slice(None)):
            return PT[r, y_hi, ahead(d, k), :, cols] + YC[q, low if high - low == 1 else low + d, :, cols].astype(F32)

        if k == 4:
            wait(R.at[0, r, 3, 0], rs_r.at[0, r, 3])
            wait(R.at[1, r, 3, 0], rs_r.at[1, r, 3])
            TS[r] = (mine(0) + R[0, r, 3, 0].astype(F32) + R[1, r, 3, 0].astype(F32)).astype(BF16)
            return
        for d in (0, 1):
            half = slice(d * hu, d * hu + hu)
            rest = slice(hu - d * hu, 2 * hu - d * hu)
            if k == 0:
                S0[d, r, :, half] = mine(d, half).astype(BF16)
                send(S0.at[d, r, :, half], R.at[d, r, 0, 0, :, half], rs_s.at[2], rs_r.at[d, r, 0], ring[d])
                continue
            if k == 1:
                wait(R.at[d, r, 0, 0, :, half], rs_r.at[d, r, 0])
                R[d, r, 0, 0, :, half] = (mine(d, half) + R[d, r, 0, 0, :, half].astype(F32)).astype(BF16)
                R[d, r, 0, 0, :, rest] = mine(d, rest).astype(BF16)
            else:
                wait(R.at[d, r, k - 1, 0], rs_r.at[d, r, k - 1])
                R[d, r, k - 1, 0] = (mine(d) + R[d, r, k - 1, 0].astype(F32)).astype(BF16)
            send(R.at[d, r, k - 1, 0], R.at[d, r, k, 0], rs_s.at[3], rs_r.at[d, r, k], ring[d])

    def hand_over(r):
        device = out_target(r)

        @pl.when(is_self(device))
        def _():
            pltpu.make_async_copy(TS.at[r], PRE.at[z], t_r).start()

        @pl.when(jnp.logical_not(is_self(device)))
        def _():
            send(TS.at[r], PRE.at[z], t_s, t_r, device)

    def pre_ticks(pair, _):
        for u in (0, 1):
            t = 2 * pair + u
            for s in (5, 4, 3, 2, 1):
                @pl.when(live(t - s, ROUNDS))
                def _(s=s, t=t, u=u):
                    (odd_step if (u - s) % 2 else even_step)(t - s, s)

            if u == 1:
                @pl.when(t == 1)
                def _(t=t):
                    service(t)

            @pl.when(t < ROUNDS)
            def _(t=t, u=u):
                wait(H.at[2 * t + 1], h_r.at[2 * t + 1])
                product(t)
                (odd_step if u else even_step)(t, 0)

            @pl.when(jnp.logical_and(t >= 1, t < ROUNDS - 1))
            def _(t=t):
                service(t + 1)

            @pl.when(t == 1)
            def _():
                ACC[...] = jnp.zeros_like(ACC)

            @pl.when(jnp.logical_and(t >= 8, t <= 10))
            def _(t=t):
                hand_over(2 * (t - 8))
                hand_over(2 * (t - 8) + 1)

            @pl.when(jnp.logical_and(t >= 11, t <= 12))
            def _(t=t):
                hand_over(t - 5)

        return 0

    lax.fori_loop(0, ROUNDS // 2 + 3, pre_ticks, 0)

    wait(PRE, t_r)
    pre = PRE[...].reshape(128, units).astype(F32)
    RES[...] = (H[0].astype(F32) + pre / (1.0 + jnp.exp(-pre))).astype(BF16)
    copy_v.wait()

    def logit_step(p, k):
        if k == 5:
            wait(LYR.at[p], ly_r.at[p])
            LF[p] = LYS[p].astype(F32) + LYR[p].astype(F32)
            return
        if k == 4:
            wait(RL.at[0, p, 3], l_r.at[0, p, 3])
            wait(RL.at[1, p, 3], l_r.at[1, p, 3])
            LYS[p] = (L[p, z] + RL[0, p, 3].astype(F32) + RL[1, p, 3].astype(F32)).astype(BF16)
            send(LYS.at[p], LYR.at[p], ly_s, ly_r.at[p], y_far)
            return
        for d in (0, 1):
            at = ahead(d, k)
            half = slice(d * hc, d * hc + hc)
            rest = slice(hc - d * hc, 2 * hc - d * hc)
            if k == 0:
                SL[d, p] = L[p, at, :, half].astype(BF16)
                send(SL.at[d, p], RL.at[d, p, 0, :, half], l_s.at[0], l_r.at[d, p, 0], ring[d])
                continue
            if k == 1:
                wait(RL.at[d, p, 0, :, half], l_r.at[d, p, 0])
                RL[d, p, 0, :, half] = (L[p, at, :, half] + RL[d, p, 0, :, half].astype(F32)).astype(BF16)
                RL[d, p, 0, :, rest] = L[p, at, :, rest].astype(BF16)
            else:
                wait(RL.at[d, p, k - 1], l_r.at[d, p, k - 1])
                RL[d, p, k - 1] = (L[p, at] + RL[d, p, k - 1].astype(F32)).astype(BF16)
            send(RL.at[d, p, k - 1], RL.at[d, p, k], l_s.at[1], l_r.at[d, p, k], ring[d])

    def logit_tick(t, _):
        @pl.when(t < PARTS)
        def _():
            cols = pl.ds(pl.multiple_of(t * vq, vq), vq)
            L[t] = jnp.dot(RES[...], V[:, cols], preferred_element_type=F32).reshape(RING, 16, vq)
            logit_step(t, 0)

        for k in (5, 4, 3, 2, 1):
            @pl.when(live(t - k, PARTS))
            def _(k=k):
                logit_step(t - k, k)

        @pl.when(t == 4)
        def _():
            again = PRE[...].reshape(128, units).astype(F32)
            sig = 1.0 / (1.0 + jnp.exp(-again))
            D1[...] = sig * (1.0 + again * (1.0 - sig))

        return 0

    lax.fori_loop(0, PARTS + 5, logit_tick, 0)

    total = jnp.zeros((16, 1), F32)
    picked = jnp.zeros((16, 1), F32)
    spot = lax.broadcasted_iota(jnp.int32, (16, 128), 0) + z * 16
    lane = lax.broadcasted_iota(jnp.int32, (16, 128), 1)
    target = jnp.sum(jnp.where(spot == lane, tgt[...], 0), axis=1, keepdims=True)
    for p in range(PARTS):
        logits = LF[p]
        hit = lax.broadcasted_iota(jnp.int32, (16, vq), 1) + p * vq == target
        total += jnp.sum(jnp.exp(logits), axis=1, keepdims=True)
        picked += jnp.sum(jnp.where(hit, logits, 0.0), axis=1, keepdims=True)

    def grad_step(p, k):
        for d in (0, 1):
            here = behind(d, k)
            half = slice(d * hc, d * hc + hc)
            if k > 0:
                piece = G.at[p, here, :, half] if k == 4 else G.at[p, here]
                wait(piece, g_r.at[d, p, k - 1])
            if k < 4:
                piece = G.at[p, here, :, half] if k == 3 else G.at[p, here]
                send(piece, piece, g_s.at[k // 3], g_r.at[d, p, k], ring[d])

    def loss_step(k):
        for d in (0, 1):
            here = behind(d, k)
            if k > 0 and (d == 0 or k < 4):
                wait(LT.at[here], lt_r.at[d, k - 1])
            if k < 3 or (k == 3 and d == 0):
                send(LT.at[here], LT.at[here], lt_s, lt_r.at[d, k], ring[d])

    for p in range(PARTS):
        hit = lax.broadcasted_iota(jnp.int32, (16, vq), 1) + p * vq == target
        G[p, z] = (jnp.exp(LF[p]) / total - jnp.where(hit, 1.0, 0.0)).astype(BF16)
        grad_step(p, 0)
    loss = jnp.log(total) - picked
    high = loss.astype(BF16).astype(F32)
    middle = (loss - high).astype(BF16).astype(F32)
    low = loss - high - middle
    LT[z] = jnp.where(
        lane == 0, high, jnp.where(lane == 1, middle, jnp.where(lane == 2, low, 0.0))
    ).astype(BF16)
    loss_step(0)

    def gradient_tick(t, _):
        for k in (3, 2, 1):
            @pl.when(live(t - k, PARTS))
            def _(k=k):
                grad_step(t - k, k)

        @pl.when(live(t - 4, PARTS))
        def _():
            p = t - 4
            grad_step(p, 4)
            cols = pl.ds(pl.multiple_of(p * vq, vq), vq)
            part = lax.dot_general(
                G[p].reshape(128, vq), V[:, cols], (((1,), (1,)), ((), ())),
                preferred_element_type=F32,
            )
            DR[...] = jnp.where(p == 0, part, DR[...] + part)

        return 0

    DR[...] = jnp.zeros_like(DR)
    lax.fori_loop(1, PARTS + 4, gradient_tick, 0)
    DQ[...] = (DR[...] * D1[...]).astype(BF16).reshape(8, 16, units)

    slot = slot_of((x + 4 - shard // 4) % 4, (y_lo + (shard // 2) % 2) % 2)
    for g in range(8):
        device = in_source(g)
        place = DP.at[slot, flip, g]

        @pl.when(is_self(device))
        def _(g=g, place=place):
            pltpu.make_async_copy(DQ.at[g], place, d_r.at[slot]).start()

        @pl.when(jnp.logical_not(is_self(device)))
        def _(g=g, place=place, device=device):
            send(DQ.at[g], place, d_s, d_r.at[slot], device)

    for k in range(1, 5):
        loss_step(k)
    column = jnp.sum(LT[...].reshape(128, 128).astype(F32), axis=1, keepdims=True)
    diagonal = lax.broadcasted_iota(jnp.int32, (128, 128), 0) == lax.broadcasted_iota(jnp.int32, (128, 128), 1)
    loss_out[...] = jnp.sum(jnp.where(diagonal, column, 0.0), axis=0, keepdims=True)

    mt = min(256, units)

    def over_y(piece, r, n):
        send(piece, piece, dy_s.at[n], dy_r.at[r], y_far)

    def even_gather(r, s):
        if s == 5:
            wait(DP.at[r, y_other], dy_r.at[r])
            return
        if s == 0:
            piece = DP.at[r, y_hi, z]
            wait(piece, d_r.at[r])
            for d in (0, 1):
                send(piece, piece, a_s.at[0], a_r.at[d, r, 0], ring[d])
            over_y(piece, r, 0)
            return
        for d in (0, 1):
            here = behind(d, s)
            piece = DP.at[r, y_hi, here]
            half = DP.at[r, y_hi, here, :, d * hu:d * hu + hu]
            if s == 4:
                wait(half, a_r.at[d, r, 3])
                continue
            wait(piece, a_r.at[d, r, s - 1])
            if s == 3:
                send(half, half, a_s.at[1], a_r.at[d, r, 3], ring[d])
            else:
                send(piece, piece, a_s.at[0], a_r.at[d, r, s], ring[d])
            over_y(piece, r, 0)
        if s == 4:
            over_y(DP.at[r, y_hi, behind(0, 4)], r, 0)

    def odd_gather(r, s):
        if s == 0:
            piece = DP.at[r, y_hi, z]
            wait(piece, d_r.at[r])
            over_y(piece, r, 1)
            return
        if s == 1:
            wait(DP.at[r, y_other, z], dy_r.at[r])
        for d in (0, 1):
            here = behind(d, s - 1)
            piece = DP.at[r, :, here]
            half = DP.at[r, d, here]
            if s == 5:
                wait(half, a_r.at[d, r, 3])
                continue
            if s > 1:
                wait(piece, a_r.at[d, r, s - 2])
            if s == 4:
                send(half, half, a_s.at[3], a_r.at[d, r, 3], ring[d])
            else:
                send(piece, piece, a_s.at[2], a_r.at[d, r, s - 1], ring[d])

    def outer(r, m):
        cols = pl.ds(pl.multiple_of(m * mt, mt), mt)
        return lax.dot_general(
            DP[r, :, :, :, cols].reshape(256, mt), H[pl.ds(2 * r, 2)].reshape(256, feats),
            (((0,), (0,)), ((), ())), preferred_element_type=F32,
        )

    def weight_ticks(pair, _):
        for u in (0, 1):
            t = 2 * pair + u
            for s in (4, 3, 2, 1, 0, 5):
                @pl.when(live(t - s, ROUNDS))
                def _(s=s, t=t, u=u):
                    (odd_gather if (u - s) % 2 else even_gather)(t - s, s)

            @pl.when(live(t - 5, ROUNDS - 1))
            def _(t=t):
                def tile(m, _):
                    rows = pl.ds(pl.multiple_of(m * mt, mt), mt)
                    ACC[rows, :] += outer(t - 5, m)
                    return 0

                lax.fori_loop(0, units // mt, tile, 0)

        return 0

    lax.fori_loop(0, ROUNDS // 2 + 3, weight_ticks, 0)

    def finish(m, _):
        rows = pl.ds(pl.multiple_of(m * mt, mt), mt)
        OUT[rows, :] = (ACC[rows, :] + outer(ROUNDS - 1, m)).astype(BF16)
        pltpu.make_async_copy(OUT.at[rows], out.at[rows], o_s).start()
        return 0

    lax.fori_loop(0, units // mt, finish, 0)

    four = DP.at[0, 0, 0:4]
    eight = DP.at[0, 0]
    wait(H.at[0:15], h_s)
    wait(eight, rs_s.at[0])
    wait(DP.at[0:3], rs_s.at[1])
    wait(four, rs_s.at[2])
    wait(DP.at[0:3, 0], rs_s.at[3])
    wait(four, y_s.at[0])
    wait(DP.at[0:2], y_s.at[1])
    wait(DP.at[0:3, 0], a_s.at[0])
    wait(four, a_s.at[1])
    wait(DP.at[0:3], a_s.at[2])
    wait(eight, a_s.at[3])
    wait(DP.at[0:2], dy_s.at[0])
    wait(four, dy_s.at[1])
    wait(SL, l_s.at[0])
    wait(RL.at[:, 0:3], l_s.at[1])
    wait(LYS, ly_s)
    wait(G.at[0:3], g_s.at[0])
    wait(G.at[0, 0:4], g_s.at[1])
    wait(LT.at[0:7], lt_s)

    @pl.when(own)
    def _():
        wait(DP.at[0, 0, 0:7], t_s)
        wait(DP.at[0, 0, 0:7], d_s)

    @pl.when(jnp.logical_not(own))
    def _():
        wait(eight, t_s)
        wait(eight, d_s)

    pltpu.make_async_copy(OUT, out, o_s).wait()


def body(hidden, head_weight, vocab_head, targets):
    feats, units = head_weight.shape
    voc = vocab_head.shape[1]
    vq = voc // PARTS
    pairs = ROUNDS // 2
    dma = pltpu.SemaphoreType.DMA
    one = pltpu.SemaphoreType.DMA
    vmem = pltpu.VMEM
    scratch = [
        vmem((2 * ROUNDS, 128, feats), BF16),
        vmem((feats, units), BF16),
        vmem((units, voc), BF16),
        vmem((ROUNDS, 2, RING, 16, units), F32),
        vmem((2, ROUNDS, 16, units), BF16),
        vmem((2, ROUNDS, 4, 2, 16, units), BF16),
        vmem((pairs, 16, units), BF16),
        vmem((pairs, 16, units), F32),
        vmem((pairs, 16, units), BF16),
        vmem((pairs, RING, 16, units), BF16),
        vmem((pairs, RING, 16, units), BF16),
        vmem((ROUNDS, 16, units), BF16),
        vmem((8, 16, units), BF16),
        vmem((128, units), BF16),
        vmem((128, units), F32),
        vmem((PARTS, RING, 16, vq), F32),
        vmem((2, PARTS, 16, vq // 2), BF16),
        vmem((2, PARTS, 4, 16, vq), BF16),
        vmem((PARTS, 16, vq), BF16),
        vmem((PARTS, 16, vq), BF16),
        vmem((PARTS, 16, vq), F32),
        vmem((PARTS, RING, 16, vq), BF16),
        vmem((RING, 16, 128), BF16),
        vmem((128, units), F32),
        vmem((8, 16, units), BF16),
        vmem((ROUNDS, 2, RING, 16, units), BF16),
        vmem((units, feats), F32),
        vmem((units, feats), BF16),
        dma((3,)),
        one, dma((2 * ROUNDS,)),
        dma((4,)), dma((2, ROUNDS, 4)),
        dma((2,)), dma((pairs,)), dma((pairs, 5)),
        one, one,
        dma((2,)), dma((2, PARTS, 4)),
        one, dma((PARTS,)),
        dma((2,)), dma((2, PARTS, 4)),
        one, dma((2, 4)),
        one, dma((ROUNDS,)),
        dma((2,)), dma((ROUNDS,)),
        dma((4,)), dma((2, ROUNDS, 4)),
        one,
    ]
    anywhere = pl.BlockSpec(memory_space=pl.ANY)
    inside = pl.BlockSpec(memory_space=pltpu.VMEM)
    grad, loss = pl.pallas_call(
        kernel,
        out_shape=[
            jax.ShapeDtypeStruct((units, feats), BF16),
            jax.ShapeDtypeStruct((1, 128), F32),
        ],
        in_specs=[anywhere, anywhere, anywhere, inside],
        out_specs=[anywhere, inside],
        scratch_shapes=scratch,
        compiler_params=pltpu.CompilerParams(
            collective_id=0, has_side_effects=True, vmem_limit_bytes=58 * 1024 * 1024
        ),
        name="head",
    )(hidden, head_weight, vocab_head, targets.reshape(1, 128))
    return grad, loss.reshape(targets.shape)


def solution(mesh):
    in_specs = (P("dp", "shard"), P("shard", "dp"), P("shard", None), P("dp"))
    out_specs = (P("dp", "shard"), P("dp"))
    return jax.shard_map(body, mesh=mesh, in_specs=in_specs, out_specs=out_specs, check_vma=False)
```

```python
import jax
import jax.numpy as jnp
from jax import lax
from jax.experimental import pallas as pl
from jax.experimental.pallas import tpu as pltpu
from jax.sharding import PartitionSpec as P

MESH = pl.DeviceIdType.MESH
BF16 = jnp.bfloat16
F32 = jnp.float32

ROUNDS = 8
RING = 8
PARTS = 4
PRE_LAG, LOGIT_LAG, GRAD_LAG, WEIGHT_LAG = 2, 4, 4, 3


def slot_of(dx, a):
    odd = dx % 2
    return odd * (2 + 2 * a + (3 - dx) // 2) + (1 - odd) * (3 * dx + a)


def offset_of(slot):
    middle = jnp.logical_and(slot >= 2, slot <= 5)
    dx = jnp.where(middle, 3 - 2 * (slot % 2), jnp.where(slot >= 6, 2, 0))
    a = jnp.where(middle, (slot // 2 + 1) % 2, slot % 2)
    return dx, a


def send(src, dst, send_sem, recv_sem, device):
    pltpu.make_async_remote_copy(
        src_ref=src,
        dst_ref=dst,
        send_sem=send_sem,
        recv_sem=recv_sem,
        device_id=device,
        device_id_type=MESH,
    ).start()


def wait(ref, sem):
    pltpu.make_async_copy(ref, ref, sem).wait()


def kernel(
    h_in, w_in, v_in, tgt, out, loss_out,
    H, W, V, PT, S0, R, YS, YK, YR, YB, YC, TS, PRE, RES, D1, L, SL, RL, LYS, LYR, LF, G, LT, DR, DQ, DP,
    ACC, OUT,
    loc, h_s, h_r, rs_s, rs_r, y_s, y_r, yc_r, t_s, t_r, l_s, l_r, ly_s, ly_r, g_s, g_r, lt_s, lt_r,
    d_s, d_r, dy_s, dy_r, a_s, a_r, o_s,
):
    dp = lax.axis_index("dp")
    shard = lax.axis_index("shard")
    x, y_lo, core = dp // 4, (dp // 2) % 2, dp % 2
    z, y_hi = shard // 2, shard % 2
    y_other = 1 - y_hi
    feats = H.shape[2]
    units = W.shape[1]
    vq = L.shape[3]
    hu, hc = units // 2, vq // 2

    x_next = ((dp + 4) % 16, shard)
    x_prev = ((dp + 12) % 16, shard)
    y_near = (dp + 2 - 4 * y_lo, shard)
    sibling = (dp + 1 - 2 * core, shard)
    z_next = (dp, (shard + 2) % 16)
    z_prev = (dp, (shard + 14) % 16)
    y_far = (dp, shard + 1 - 2 * y_hi)
    ring = (z_next, z_prev)

    def out_target(slot):
        dx, a = offset_of(slot)
        there = ((x + dx) % 4) * 4 + ((y_lo + a) % 2) * 2 + (core + y_hi) % 2
        return (there, dp)

    flip = (core + shard % 2) % 2

    def in_source(g):
        return (shard, 2 * g + flip)

    def is_self(device):
        return jnp.logical_and(device[0] == dp, device[1] == shard)

    own = jnp.logical_and(dp == shard, y_hi == 0)

    barrier = pltpu.get_barrier_semaphore()
    near = (x_next, x_prev, y_near, sibling, z_next, z_prev, y_far)
    for device in near:
        pl.semaphore_signal(barrier, inc=1, device_id=device, device_id_type=MESH)
    copy_w = pltpu.make_async_copy(w_in, W, loc.at[0])
    copy_w.start()
    copy_h = pltpu.make_async_copy(h_in, H.at[0], loc.at[2])
    copy_h.start()
    copy_v = pltpu.make_async_copy(v_in, V, loc.at[1])
    pl.semaphore_wait(barrier, len(near))

    def pass_on(src, slot, device):
        send(src, H.at[slot], h_s, h_r.at[slot], device)

    pass_on(h_in, 1, sibling)
    pass_on(h_in, 2, y_near)
    pass_on(h_in, 4, x_next)
    pass_on(h_in, 6, x_prev)
    copy_v.start()

    def service(q):
        wait(H.at[2 * q], h_r.at[2 * q])
        pass_on(H.at[2 * q], 2 * q + 1, sibling)

        @pl.when(q == 1)
        def _():
            pass_on(H.at[2], 8, x_next)
            pass_on(H.at[2], 10, x_prev)

        @pl.when(q == 2)
        def _():
            pass_on(H.at[4], 12, x_next)

        @pl.when(q == 5)
        def _():
            pass_on(H.at[10], 14, x_prev)

    copy_h.wait()
    copy_w.wait()

    def ahead(d, k):
        return (z + (RING // 2 - k if d == 0 else RING // 2 + k)) % RING

    def behind(d, k):
        return (z + (RING - k if d == 0 else k)) % RING

    def live(r, n):
        return jnp.logical_and(r >= 0, r < n)

    nt = min(512, units)

    def product(t):
        def tile(n, _):
            cols = pl.ds(pl.multiple_of(n * nt, nt), nt)
            rows = H[pl.ds(2 * t, 2)].reshape(256, feats)
            PT[t, :, :, :, cols] = jnp.dot(
                rows, W[:, cols], preferred_element_type=F32
            ).reshape(2, RING, 16, nt)
            return 0

        lax.fori_loop(0, units // nt, tile, 0)

    def even_step(r, s):
        q = r // 2
        if s == 0:
            for d in (0, 1):
                S0[d, r] = PT[r, d, ahead(d, 0)].astype(BF16)
                send(S0.at[d, r], R.at[d, r, 0, d], rs_s.at[0], rs_r.at[d, r, 0], ring[d])
        elif s < 4:
            for d in (0, 1):
                at = ahead(d, s)
                if s == 1:
                    wait(R.at[d, r, 0, d], rs_r.at[d, r, 0])
                    R[d, r, 0, d] = (PT[r, d, at] + R[d, r, 0, d].astype(F32)).astype(BF16)
                    R[d, r, 0, 1 - d] = PT[r, 1 - d, at].astype(BF16)
                else:
                    wait(R.at[d, r, s - 1], rs_r.at[d, r, s - 1])
                    R[d, r, s - 1] = (PT[r, :, at] + R[d, r, s - 1].astype(F32)).astype(BF16)
                send(R.at[d, r, s - 1], R.at[d, r, s], rs_s.at[1], rs_r.at[d, r, s], ring[d])
        elif s == 4:
            wait(R.at[0, r, 3], rs_r.at[0, r, 3])
            wait(R.at[1, r, 3], rs_r.at[1, r, 3])

            def total(h):
                return PT[r, h, z] + R[0, r, 3, h].astype(F32) + R[1, r, 3, h].astype(F32)

            YS[q] = total(y_other).astype(BF16)
            send(YS.at[q], YR.at[q], y_s.at[0], y_r.at[q], y_far)
            YK[q] = total(y_hi)
        else:
            wait(YR.at[q], y_r.at[q])
            TS[r] = (YK[q] + YR[q].astype(F32)).astype(BF16)

    groups = ((0, 1), (1, 3), (3, 5), (5, 7), (7, 8))

    def odd_step(r, s):
        q = r // 2
        if s == 0:
            for n, (low, high) in enumerate(groups):
                YB[q, low] = PT[r, y_other, ahead(0, n)].astype(BF16)
                if high - low == 2:
                    YB[q, low + 1] = PT[r, y_other, ahead(1, n)].astype(BF16)
                send(YB.at[q, low:high], YC.at[q, low:high], y_s.at[1], yc_r.at[q, n], y_far)
            return
        k = s - 1
        low, high = groups[k]
        wait(YC.at[q, low:high], yc_r.at[q, k])

        def mine(d, cols=slice(None)):
            return PT[r, y_hi, ahead(d, k), :, cols] + YC[q, low if high - low == 1 else low + d, :, cols].astype(F32)

        if k == 4:
            wait(R.at[0, r, 3, 0], rs_r.at[0, r, 3])
            wait(R.at[1, r, 3, 0], rs_r.at[1, r, 3])
            TS[r] = (mine(0) + R[0, r, 3, 0].astype(F32) + R[1, r, 3, 0].astype(F32)).astype(BF16)
            return
        for d in (0, 1):
            half = slice(d * hu, d * hu + hu)
            rest = slice(hu - d * hu, 2 * hu - d * hu)
            if k == 0:
                S0[d, r, :, half] = mine(d, half).astype(BF16)
                send(S0.at[d, r, :, half], R.at[d, r, 0, 0, :, half], rs_s.at[2], rs_r.at[d, r, 0], ring[d])
                continue
            if k == 1:
                wait(R.at[d, r, 0, 0, :, half], rs_r.at[d, r, 0])
                R[d, r, 0, 0, :, half] = (mine(d, half) + R[d, r, 0, 0, :, half].astype(F32)).astype(BF16)
                R[d, r, 0, 0, :, rest] = mine(d, rest).astype(BF16)
            else:
                wait(R.at[d, r, k - 1, 0], rs_r.at[d, r, k - 1])
                R[d, r, k - 1, 0] = (mine(d) + R[d, r, k - 1, 0].astype(F32)).astype(BF16)
            send(R.at[d, r, k - 1, 0], R.at[d, r, k, 0], rs_s.at[3], rs_r.at[d, r, k], ring[d])

    def hand_over(r):
        device = out_target(r)

        @pl.when(is_self(device))
        def _():
            pltpu.make_async_copy(TS.at[r], PRE.at[z], t_r).start()

        @pl.when(jnp.logical_not(is_self(device)))
        def _():
            send(TS.at[r], PRE.at[z], t_s, t_r, device)

    def pre_ticks(pair, _):
        for u in (0, 1):
            t = 2 * pair + u
            for s in (5, 4, 3, 2, 1):
                @pl.when(live(t - PRE_LAG * s, ROUNDS))
                def _(s=s, t=t, u=u):
                    (odd_step if (u - PRE_LAG * s) % 2 else even_step)(t - PRE_LAG * s, s)

            if u == 1:
                @pl.when(t == 1)
                def _(t=t):
                    service(t)

            @pl.when(t < ROUNDS)
            def _(t=t, u=u):
                wait(H.at[2 * t + 1], h_r.at[2 * t + 1])
                product(t)
                (odd_step if u else even_step)(t, 0)

            @pl.when(jnp.logical_and(t >= 1, t < ROUNDS - 1))
            def _(t=t):
                service(t + 1)

            @pl.when(t == 1)
            def _():
                ACC[...] = jnp.zeros_like(ACC)

            e = t - 5 * (PRE_LAG - 1)

            @pl.when(jnp.logical_and(e >= 8, e <= 10))
            def _(e=e):
                hand_over(2 * (e - 8))
                hand_over(2 * (e - 8) + 1)

            @pl.when(jnp.logical_and(e >= 11, e <= 12))
            def _(e=e):
                hand_over(e - 5)

        return 0

    lax.fori_loop(0, (ROUNDS + 5 * PRE_LAG + 1) // 2, pre_ticks, 0)

    wait(PRE, t_r)
    pre = PRE[...].reshape(128, units).astype(F32)
    RES[...] = (H[0].astype(F32) + pre / (1.0 + jnp.exp(-pre))).astype(BF16)
    copy_v.wait()

    def logit_step(p, k):
        if k == 5:
            wait(LYR.at[p], ly_r.at[p])
            LF[p] = LYS[p].astype(F32) + LYR[p].astype(F32)
            return
        if k == 4:
            wait(RL.at[0, p, 3], l_r.at[0, p, 3])
            wait(RL.at[1, p, 3], l_r.at[1, p, 3])
            LYS[p] = (L[p, z] + RL[0, p, 3].astype(F32) + RL[1, p, 3].astype(F32)).astype(BF16)
            send(LYS.at[p], LYR.at[p], ly_s, ly_r.at[p], y_far)
            return
        for d in (0, 1):
            at = ahead(d, k)
            half = slice(d * hc, d * hc + hc)
            rest = slice(hc - d * hc, 2 * hc - d * hc)
            if k == 0:
                SL[d, p] = L[p, at, :, half].astype(BF16)
                send(SL.at[d, p], RL.at[d, p, 0, :, half], l_s.at[0], l_r.at[d, p, 0], ring[d])
                continue
            if k == 1:
                wait(RL.at[d, p, 0, :, half], l_r.at[d, p, 0])
                RL[d, p, 0, :, half] = (L[p, at, :, half] + RL[d, p, 0, :, half].astype(F32)).astype(BF16)
                RL[d, p, 0, :, rest] = L[p, at, :, rest].astype(BF16)
            else:
                wait(RL.at[d, p, k - 1], l_r.at[d, p, k - 1])
                RL[d, p, k - 1] = (L[p, at] + RL[d, p, k - 1].astype(F32)).astype(BF16)
            send(RL.at[d, p, k - 1], RL.at[d, p, k], l_s.at[1], l_r.at[d, p, k], ring[d])

    def logit_tick(t, _):
        @pl.when(t < PARTS)
        def _():
            cols = pl.ds(pl.multiple_of(t * vq, vq), vq)
            L[t] = jnp.dot(RES[...], V[:, cols], preferred_element_type=F32).reshape(RING, 16, vq)
            logit_step(t, 0)

        for k in (5, 4, 3, 2, 1):
            @pl.when(live(t - LOGIT_LAG * k, PARTS))
            def _(k=k):
                logit_step(t - LOGIT_LAG * k, k)

        @pl.when(t == 4)
        def _():
            again = PRE[...].reshape(128, units).astype(F32)
            sig = 1.0 / (1.0 + jnp.exp(-again))
            D1[...] = sig * (1.0 + again * (1.0 - sig))

        return 0

    lax.fori_loop(0, PARTS + 5 * LOGIT_LAG, logit_tick, 0)

    total = jnp.zeros((16, 1), F32)
    picked = jnp.zeros((16, 1), F32)
    spot = lax.broadcasted_iota(jnp.int32, (16, 128), 0) + z * 16
    lane = lax.broadcasted_iota(jnp.int32, (16, 128), 1)
    target = jnp.sum(jnp.where(spot == lane, tgt[...], 0), axis=1, keepdims=True)
    for p in range(PARTS):
        logits = LF[p]
        hit = lax.broadcasted_iota(jnp.int32, (16, vq), 1) + p * vq == target
        total += jnp.sum(jnp.exp(logits), axis=1, keepdims=True)
        picked += jnp.sum(jnp.where(hit, logits, 0.0), axis=1, keepdims=True)

    def grad_step(p, k):
        for d in (0, 1):
            here = behind(d, k)
            half = slice(d * hc, d * hc + hc)
            if k > 0:
                piece = G.at[p, here, :, half] if k == 4 else G.at[p, here]
                wait(piece, g_r.at[d, p, k - 1])
            if k < 4:
                piece = G.at[p, here, :, half] if k == 3 else G.at[p, here]
                send(piece, piece, g_s.at[k // 3], g_r.at[d, p, k], ring[d])

    def loss_step(k):
        for d in (0, 1):
            here = behind(d, k)
            if k > 0 and (d == 0 or k < 4):
                wait(LT.at[here], lt_r.at[d, k - 1])
            if k < 3 or (k == 3 and d == 0):
                send(LT.at[here], LT.at[here], lt_s, lt_r.at[d, k], ring[d])

    for p in range(PARTS):
        hit = lax.broadcasted_iota(jnp.int32, (16, vq), 1) + p * vq == target
        G[p, z] = (jnp.exp(LF[p]) / total - jnp.where(hit, 1.0, 0.0)).astype(BF16)
        grad_step(p, 0)
    loss = jnp.log(total) - picked
    high = loss.astype(BF16).astype(F32)
    middle = (loss - high).astype(BF16).astype(F32)
    low = loss - high - middle
    LT[z] = jnp.where(
        lane == 0, high, jnp.where(lane == 1, middle, jnp.where(lane == 2, low, 0.0))
    ).astype(BF16)
    loss_step(0)

    def gradient_tick(t, _):
        for k in (3, 2, 1):
            @pl.when(live(t - GRAD_LAG * k, PARTS))
            def _(k=k):
                grad_step(t - GRAD_LAG * k, k)

        @pl.when(live(t - 4 * GRAD_LAG, PARTS))
        def _():
            p = t - 4 * GRAD_LAG
            grad_step(p, 4)
            cols = pl.ds(pl.multiple_of(p * vq, vq), vq)
            part = lax.dot_general(
                G[p].reshape(128, vq), V[:, cols], (((1,), (1,)), ((), ())),
                preferred_element_type=F32,
            )
            DR[...] = jnp.where(p == 0, part, DR[...] + part)

        return 0

    DR[...] = jnp.zeros_like(DR)
    lax.fori_loop(1, PARTS + 4 * GRAD_LAG, gradient_tick, 0)
    DQ[...] = (DR[...] * D1[...]).astype(BF16).reshape(8, 16, units)

    slot = slot_of((x + 4 - shard // 4) % 4, (y_lo + (shard // 2) % 2) % 2)
    for g in range(8):
        device = in_source(g)
        place = DP.at[slot, flip, g]

        @pl.when(is_self(device))
        def _(g=g, place=place):
            pltpu.make_async_copy(DQ.at[g], place, d_r.at[slot]).start()

        @pl.when(jnp.logical_not(is_self(device)))
        def _(g=g, place=place, device=device):
            send(DQ.at[g], place, d_s, d_r.at[slot], device)

    for k in range(1, 5):
        loss_step(k)
    column = jnp.sum(LT[...].reshape(128, 128).astype(F32), axis=1, keepdims=True)
    diagonal = lax.broadcasted_iota(jnp.int32, (128, 128), 0) == lax.broadcasted_iota(jnp.int32, (128, 128), 1)
    loss_out[...] = jnp.sum(jnp.where(diagonal, column, 0.0), axis=0, keepdims=True)

    mt = min(256, units)

    def over_y(piece, r, n):
        send(piece, piece, dy_s.at[n], dy_r.at[r], y_far)

    def even_gather(r, s):
        if s == 5:
            wait(DP.at[r, y_other], dy_r.at[r])
            return
        if s == 0:
            piece = DP.at[r, y_hi, z]
            wait(piece, d_r.at[r])
            for d in (0, 1):
                send(piece, piece, a_s.at[0], a_r.at[d, r, 0], ring[d])
            over_y(piece, r, 0)
            return
        for d in (0, 1):
            here = behind(d, s)
            piece = DP.at[r, y_hi, here]
            half = DP.at[r, y_hi, here, :, d * hu:d * hu + hu]
            if s == 4:
                wait(half, a_r.at[d, r, 3])
                continue
            wait(piece, a_r.at[d, r, s - 1])
            if s == 3:
                send(half, half, a_s.at[1], a_r.at[d, r, 3], ring[d])
            else:
                send(piece, piece, a_s.at[0], a_r.at[d, r, s], ring[d])
            over_y(piece, r, 0)
        if s == 4:
            over_y(DP.at[r, y_hi, behind(0, 4)], r, 0)

    def odd_gather(r, s):
        if s == 0:
            piece = DP.at[r, y_hi, z]
            wait(piece, d_r.at[r])
            over_y(piece, r, 1)
            return
        if s == 1:
            wait(DP.at[r, y_other, z], dy_r.at[r])
        for d in (0, 1):
            here = behind(d, s - 1)
            piece = DP.at[r, :, here]
            half = DP.at[r, d, here]
            if s == 5:
                wait(half, a_r.at[d, r, 3])
                continue
            if s > 1:
                wait(piece, a_r.at[d, r, s - 2])
            if s == 4:
                send(half, half, a_s.at[3], a_r.at[d, r, 3], ring[d])
            else:
                send(piece, piece, a_s.at[2], a_r.at[d, r, s - 1], ring[d])

    def outer(r, m):
        cols = pl.ds(pl.multiple_of(m * mt, mt), mt)
        return lax.dot_general(
            DP[r, :, :, :, cols].reshape(256, mt), H[pl.ds(2 * r, 2)].reshape(256, feats),
            (((0,), (0,)), ((), ())), preferred_element_type=F32,
        )

    def weight_ticks(pair, _):
        for u in (0, 1):
            t = 2 * pair + u
            for s in (4, 3, 2, 1, 0, 5):
                @pl.when(live(t - WEIGHT_LAG * s, ROUNDS))
                def _(s=s, t=t, u=u):
                    (odd_gather if (u - WEIGHT_LAG * s) % 2 else even_gather)(t - WEIGHT_LAG * s, s)

            @pl.when(live(t - 5 * WEIGHT_LAG, ROUNDS - 1))
            def _(t=t):
                def tile(m, _):
                    rows = pl.ds(pl.multiple_of(m * mt, mt), mt)
                    ACC[rows, :] += outer(t - 5 * WEIGHT_LAG, m)
                    return 0

                lax.fori_loop(0, units // mt, tile, 0)

        return 0

    lax.fori_loop(0, (ROUNDS + 5 * WEIGHT_LAG + 1) // 2, weight_ticks, 0)

    def finish(m, _):
        rows = pl.ds(pl.multiple_of(m * mt, mt), mt)
        OUT[rows, :] = (ACC[rows, :] + outer(ROUNDS - 1, m)).astype(BF16)
        pltpu.make_async_copy(OUT.at[rows], out.at[rows], o_s).start()
        return 0

    lax.fori_loop(0, units // mt, finish, 0)

    four = DP.at[0, 0, 0:4]
    eight = DP.at[0, 0]
    wait(H.at[0:15], h_s)
    wait(eight, rs_s.at[0])
    wait(DP.at[0:3], rs_s.at[1])
    wait(four, rs_s.at[2])
    wait(DP.at[0:3, 0], rs_s.at[3])
    wait(four, y_s.at[0])
    wait(DP.at[0:2], y_s.at[1])
    wait(DP.at[0:3, 0], a_s.at[0])
    wait(four, a_s.at[1])
    wait(DP.at[0:3], a_s.at[2])
    wait(eight, a_s.at[3])
    wait(DP.at[0:2], dy_s.at[0])
    wait(four, dy_s.at[1])
    wait(SL, l_s.at[0])
    wait(RL.at[:, 0:3], l_s.at[1])
    wait(LYS, ly_s)
    wait(G.at[0:3], g_s.at[0])
    wait(G.at[0, 0:4], g_s.at[1])
    wait(LT.at[0:7], lt_s)

    @pl.when(own)
    def _():
        wait(DP.at[0, 0, 0:7], t_s)
        wait(DP.at[0, 0, 0:7], d_s)

    @pl.when(jnp.logical_not(own))
    def _():
        wait(eight, t_s)
        wait(eight, d_s)

    pltpu.make_async_copy(OUT, out, o_s).wait()


def body(hidden, head_weight, vocab_head, targets):
    feats, units = head_weight.shape
    voc = vocab_head.shape[1]
    vq = voc // PARTS
    pairs = ROUNDS // 2
    dma = pltpu.SemaphoreType.DMA
    one = pltpu.SemaphoreType.DMA
    vmem = pltpu.VMEM
    scratch = [
        vmem((2 * ROUNDS, 128, feats), BF16),
        vmem((feats, units), BF16),
        vmem((units, voc), BF16),
        vmem((ROUNDS, 2, RING, 16, units), F32),
        vmem((2, ROUNDS, 16, units), BF16),
        vmem((2, ROUNDS, 4, 2, 16, units), BF16),
        vmem((pairs, 16, units), BF16),
        vmem((pairs, 16, units), F32),
        vmem((pairs, 16, units), BF16),
        vmem((pairs, RING, 16, units), BF16),
        vmem((pairs, RING, 16, units), BF16),
        vmem((ROUNDS, 16, units), BF16),
        vmem((8, 16, units), BF16),
        vmem((128, units), BF16),
        vmem((128, units), F32),
        vmem((PARTS, RING, 16, vq), F32),
        vmem((2, PARTS, 16, vq // 2), BF16),
        vmem((2, PARTS, 4, 16, vq), BF16),
        vmem((PARTS, 16, vq), BF16),
        vmem((PARTS, 16, vq), BF16),
        vmem((PARTS, 16, vq), F32),
        vmem((PARTS, RING, 16, vq), BF16),
        vmem((RING, 16, 128), BF16),
        vmem((128, units), F32),
        vmem((8, 16, units), BF16),
        vmem((ROUNDS, 2, RING, 16, units), BF16),
        vmem((units, feats), F32),
        vmem((units, feats), BF16),
        dma((3,)),
        one, dma((2 * ROUNDS,)),
        dma((4,)), dma((2, ROUNDS, 4)),
        dma((2,)), dma((pairs,)), dma((pairs, 5)),
        one, one,
        dma((2,)), dma((2, PARTS, 4)),
        one, dma((PARTS,)),
        dma((2,)), dma((2, PARTS, 4)),
        one, dma((2, 4)),
        one, dma((ROUNDS,)),
        dma((2,)), dma((ROUNDS,)),
        dma((4,)), dma((2, ROUNDS, 4)),
        one,
    ]
    anywhere = pl.BlockSpec(memory_space=pl.ANY)
    inside = pl.BlockSpec(memory_space=pltpu.VMEM)
    grad, loss = pl.pallas_call(
        kernel,
        out_shape=[
            jax.ShapeDtypeStruct((units, feats), BF16),
            jax.ShapeDtypeStruct((1, 128), F32),
        ],
        in_specs=[anywhere, anywhere, anywhere, inside],
        out_specs=[anywhere, inside],
        scratch_shapes=scratch,
        compiler_params=pltpu.CompilerParams(
            collective_id=0, has_side_effects=True, vmem_limit_bytes=58 * 1024 * 1024
        ),
        name="head",
    )(hidden, head_weight, vocab_head, targets.reshape(1, 128))
    return grad, loss.reshape(targets.shape)


def solution(mesh):
    in_specs = (P("dp", "shard"), P("shard", "dp"), P("shard", None), P("dp"))
    out_specs = (P("dp", "shard"), P("dp"))
    return jax.shard_map(body, mesh=mesh, in_specs=in_specs, out_specs=out_specs, check_vma=False)
```

```python
import jax
import jax.numpy as jnp
from jax import lax
from jax.experimental import pallas as pl
from jax.experimental.pallas import tpu as pltpu
from jax.sharding import PartitionSpec as P

MESH = pl.DeviceIdType.MESH
BF16 = jnp.bfloat16
F32 = jnp.float32

ROUNDS = 8
RING = 8
PARTS = 4
PRE_LAG, LOGIT_LAG, GRAD_LAG, WEIGHT_LAG = 2, 4, 4, 3


def slot_of(dx, a):
    odd = dx % 2
    return odd * (2 + 2 * a + (3 - dx) // 2) + (1 - odd) * (3 * dx + a)


def offset_of(slot):
    middle = jnp.logical_and(slot >= 2, slot <= 5)
    dx = jnp.where(middle, 3 - 2 * (slot % 2), jnp.where(slot >= 6, 2, 0))
    a = jnp.where(middle, (slot // 2 + 1) % 2, slot % 2)
    return dx, a


def send(src, dst, send_sem, recv_sem, device):
    pltpu.make_async_remote_copy(
        src_ref=src,
        dst_ref=dst,
        send_sem=send_sem,
        recv_sem=recv_sem,
        device_id=device,
        device_id_type=MESH,
    ).start()


def wait(ref, sem):
    pltpu.make_async_copy(ref, ref, sem).wait()


def kernel(
    h_in, w_in, v_in, tgt, out, loss_out,
    H, W, V, PT, S0, R, YS, YK, YR, YB, YC, TS, TM, PRE, RES, D1, L, SL, RL, LYS, LYR, LF, G, LT, DR, DQ, DP,
    ACC, OUT,
    loc, h_s, h_r, rs_s, rs_r, y_s, y_r, yc_r, m_s, m_r, t_s, t_r, l_s, l_r, ly_s, ly_r, g_s, g_r, lt_s, lt_r,
    d_s, d_r, dy_s, dy_r, a_s, a_r, o_s,
):
    dp = lax.axis_index("dp")
    shard = lax.axis_index("shard")
    x, y_lo, core = dp // 4, (dp // 2) % 2, dp % 2
    z, y_hi = shard // 2, shard % 2
    y_other = 1 - y_hi
    feats = H.shape[2]
    units = W.shape[1]
    vq = L.shape[3]
    hu, hc = units // 2, vq // 2

    x_next = ((dp + 4) % 16, shard)
    x_prev = ((dp + 12) % 16, shard)
    y_near = (dp + 2 - 4 * y_lo, shard)
    sibling = (dp + 1 - 2 * core, shard)
    z_next = (dp, (shard + 2) % 16)
    z_prev = (dp, (shard + 14) % 16)
    y_far = (dp, shard + 1 - 2 * y_hi)
    ring = (z_next, z_prev)

    def out_target(slot):
        dx, a = offset_of(slot)
        there = ((x + dx) % 4) * 4 + ((y_lo + a) % 2) * 2 + (core + y_hi) % 2
        return (there, shard)

    def in_column(slot):
        dx, a = offset_of(slot)
        column = ((x + 4 - dx) % 4) * 4 + ((y_lo + a) % 2) * 2 + (core + y_hi) % 2
        return (dp, column)

    flip = (core + shard % 2) % 2

    def in_source(g):
        return (shard, 2 * g + flip)

    def is_self(device):
        return jnp.logical_and(device[0] == dp, device[1] == shard)

    own = jnp.logical_and(dp == shard, y_hi == 0)

    barrier = pltpu.get_barrier_semaphore()
    near = (x_next, x_prev, y_near, sibling, z_next, z_prev, y_far)
    for device in near:
        pl.semaphore_signal(barrier, inc=1, device_id=device, device_id_type=MESH)
    copy_w = pltpu.make_async_copy(w_in, W, loc.at[0])
    copy_w.start()
    copy_h = pltpu.make_async_copy(h_in, H.at[0], loc.at[2])
    copy_h.start()
    copy_v = pltpu.make_async_copy(v_in, V, loc.at[1])
    pl.semaphore_wait(barrier, len(near))

    def pass_on(src, slot, device):
        send(src, H.at[slot], h_s, h_r.at[slot], device)

    pass_on(h_in, 1, sibling)
    pass_on(h_in, 2, y_near)
    pass_on(h_in, 4, x_next)
    pass_on(h_in, 6, x_prev)
    copy_v.start()

    def service(q):
        wait(H.at[2 * q], h_r.at[2 * q])
        pass_on(H.at[2 * q], 2 * q + 1, sibling)

        @pl.when(q == 1)
        def _():
            pass_on(H.at[2], 8, x_next)
            pass_on(H.at[2], 10, x_prev)

        @pl.when(q == 2)
        def _():
            pass_on(H.at[4], 12, x_next)

        @pl.when(q == 5)
        def _():
            pass_on(H.at[10], 14, x_prev)

    copy_h.wait()
    copy_w.wait()

    def ahead(d, k):
        return (z + (RING // 2 - k if d == 0 else RING // 2 + k)) % RING

    def behind(d, k):
        return (z + (RING - k if d == 0 else k)) % RING

    def live(r, n):
        return jnp.logical_and(r >= 0, r < n)

    nt = min(512, units)

    def product(t):
        def tile(n, _):
            cols = pl.ds(pl.multiple_of(n * nt, nt), nt)
            rows = H[pl.ds(2 * t, 2)].reshape(256, feats)
            PT[t, :, :, :, cols] = jnp.dot(
                rows, W[:, cols], preferred_element_type=F32
            ).reshape(2, RING, 16, nt)
            return 0

        lax.fori_loop(0, units // nt, tile, 0)

    def even_step(r, s):
        q = r // 2
        if s == 0:
            for d in (0, 1):
                S0[d, r] = PT[r, d, ahead(d, 0)].astype(BF16)
                send(S0.at[d, r], R.at[d, r, 0, d], rs_s.at[0], rs_r.at[d, r, 0], ring[d])
        elif s < 4:
            for d in (0, 1):
                at = ahead(d, s)
                if s == 1:
                    wait(R.at[d, r, 0, d], rs_r.at[d, r, 0])
                    R[d, r, 0, d] = (PT[r, d, at] + R[d, r, 0, d].astype(F32)).astype(BF16)
                    R[d, r, 0, 1 - d] = PT[r, 1 - d, at].astype(BF16)
                else:
                    wait(R.at[d, r, s - 1], rs_r.at[d, r, s - 1])
                    R[d, r, s - 1] = (PT[r, :, at] + R[d, r, s - 1].astype(F32)).astype(BF16)
                send(R.at[d, r, s - 1], R.at[d, r, s], rs_s.at[1], rs_r.at[d, r, s], ring[d])
        elif s == 4:
            wait(R.at[0, r, 3], rs_r.at[0, r, 3])
            wait(R.at[1, r, 3], rs_r.at[1, r, 3])

            def total(h):
                return PT[r, h, z] + R[0, r, 3, h].astype(F32) + R[1, r, 3, h].astype(F32)

            YS[q] = total(y_other).astype(BF16)
            send(YS.at[q], YR.at[q], y_s.at[0], y_r.at[q], y_far)
            YK[q] = total(y_hi)
        else:
            wait(YR.at[q], y_r.at[q])
            TS[r] = (YK[q] + YR[q].astype(F32)).astype(BF16)

    groups = ((0, 1), (1, 3), (3, 5), (5, 7), (7, 8))

    def odd_step(r, s):
        q = r // 2
        if s == 0:
            for n, (low, high) in enumerate(groups):
                YB[q, low] = PT[r, y_other, ahead(0, n)].astype(BF16)
                if high - low == 2:
                    YB[q, low + 1] = PT[r, y_other, ahead(1, n)].astype(BF16)
                send(YB.at[q, low:high], YC.at[q, low:high], y_s.at[1], yc_r.at[q, n], y_far)
            return
        k = s - 1
        low, high = groups[k]
        wait(YC.at[q, low:high], yc_r.at[q, k])

        def mine(d, cols=slice(None)):
            return PT[r, y_hi, ahead(d, k), :, cols] + YC[q, low if high - low == 1 else low + d, :, cols].astype(F32)

        if k == 4:
            wait(R.at[0, r, 3, 0], rs_r.at[0, r, 3])
            wait(R.at[1, r, 3, 0], rs_r.at[1, r, 3])
            TS[r] = (mine(0) + R[0, r, 3, 0].astype(F32) + R[1, r, 3, 0].astype(F32)).astype(BF16)
            return
        for d in (0, 1):
            half = slice(d * hu, d * hu + hu)
            rest = slice(hu - d * hu, 2 * hu - d * hu)
            if k == 0:
                S0[d, r, :, half] = mine(d, half).astype(BF16)
                send(S0.at[d, r, :, half], R.at[d, r, 0, 0, :, half], rs_s.at[2], rs_r.at[d, r, 0], ring[d])
                continue
            if k == 1:
                wait(R.at[d, r, 0, 0, :, half], rs_r.at[d, r, 0])
                R[d, r, 0, 0, :, half] = (mine(d, half) + R[d, r, 0, 0, :, half].astype(F32)).astype(BF16)
                R[d, r, 0, 0, :, rest] = mine(d, rest).astype(BF16)
            else:
                wait(R.at[d, r, k - 1, 0], rs_r.at[d, r, k - 1])
                R[d, r, k - 1, 0] = (mine(d) + R[d, r, k - 1, 0].astype(F32)).astype(BF16)
            send(R.at[d, r, k - 1, 0], R.at[d, r, k, 0], rs_s.at[3], rs_r.at[d, r, k], ring[d])

    def move(src, dst, send_sem, recv_sem, device):
        @pl.when(is_self(device))
        def _():
            pltpu.make_async_copy(src, dst, recv_sem).start()

        @pl.when(jnp.logical_not(is_self(device)))
        def _():
            send(src, dst, send_sem, recv_sem, device)

    def to_tokens(r):
        move(TS.at[r], TM.at[r], m_s, m_r.at[r], out_target(r))

    def to_features(r):
        wait(TM.at[r], m_r.at[r])
        move(TM.at[r], PRE.at[z], t_s, t_r, in_column(r))

    def pre_ticks(pair, _):
        for u in (0, 1):
            t = 2 * pair + u
            for s in (5, 4, 3, 2, 1):
                @pl.when(live(t - PRE_LAG * s, ROUNDS))
                def _(s=s, t=t, u=u):
                    (odd_step if (u - PRE_LAG * s) % 2 else even_step)(t - PRE_LAG * s, s)
                    if s == 5:
                        to_tokens(t - PRE_LAG * s)

            if u == 1:
                @pl.when(t == 1)
                def _(t=t):
                    service(t)

            @pl.when(t < ROUNDS)
            def _(t=t, u=u):
                wait(H.at[2 * t + 1], h_r.at[2 * t + 1])
                product(t)
                (odd_step if u else even_step)(t, 0)

            @pl.when(jnp.logical_and(t >= 1, t < ROUNDS - 1))
            def _(t=t):
                service(t + 1)

            @pl.when(t == 1)
            def _():
                ACC[...] = jnp.zeros_like(ACC)

            e = t - 5 * (PRE_LAG - 1)

            @pl.when(jnp.logical_and(e >= 9, e <= 11))
            def _(e=e):
                to_features(2 * (e - 9))
                to_features(2 * (e - 9) + 1)

            @pl.when(e == 12)
            def _():
                to_features(6)

        return 0

    lax.fori_loop(0, (ROUNDS + 5 * PRE_LAG + 1) // 2, pre_ticks, 0)

    to_features(7)
    wait(PRE, t_r)
    pre = PRE[...].reshape(128, units).astype(F32)
    RES[...] = (H[0].astype(F32) + pre / (1.0 + jnp.exp(-pre))).astype(BF16)
    copy_v.wait()

    def logit_step(p, k):
        if k == 5:
            wait(LYR.at[p], ly_r.at[p])
            LF[p] = LYS[p].astype(F32) + LYR[p].astype(F32)
            return
        if k == 4:
            wait(RL.at[0, p, 3], l_r.at[0, p, 3])
            wait(RL.at[1, p, 3], l_r.at[1, p, 3])
            LYS[p] = (L[p, z] + RL[0, p, 3].astype(F32) + RL[1, p, 3].astype(F32)).astype(BF16)
            send(LYS.at[p], LYR.at[p], ly_s, ly_r.at[p], y_far)
            return
        for d in (0, 1):
            at = ahead(d, k)
            half = slice(d * hc, d * hc + hc)
            rest = slice(hc - d * hc, 2 * hc - d * hc)
            if k == 0:
                SL[d, p] = L[p, at, :, half].astype(BF16)
                send(SL.at[d, p], RL.at[d, p, 0, :, half], l_s.at[0], l_r.at[d, p, 0], ring[d])
                continue
            if k == 1:
                wait(RL.at[d, p, 0, :, half], l_r.at[d, p, 0])
                RL[d, p, 0, :, half] = (L[p, at, :, half] + RL[d, p, 0, :, half].astype(F32)).astype(BF16)
                RL[d, p, 0, :, rest] = L[p, at, :, rest].astype(BF16)
            else:
                wait(RL.at[d, p, k - 1], l_r.at[d, p, k - 1])
                RL[d, p, k - 1] = (L[p, at] + RL[d, p, k - 1].astype(F32)).astype(BF16)
            send(RL.at[d, p, k - 1], RL.at[d, p, k], l_s.at[1], l_r.at[d, p, k], ring[d])

    def logit_tick(t, _):
        @pl.when(t < PARTS)
        def _():
            cols = pl.ds(pl.multiple_of(t * vq, vq), vq)
            L[t] = jnp.dot(RES[...], V[:, cols], preferred_element_type=F32).reshape(RING, 16, vq)
            logit_step(t, 0)

        for k in (5, 4, 3, 2, 1):
            @pl.when(live(t - LOGIT_LAG * k, PARTS))
            def _(k=k):
                logit_step(t - LOGIT_LAG * k, k)

        @pl.when(t == 4)
        def _():
            again = PRE[...].reshape(128, units).astype(F32)
            sig = 1.0 / (1.0 + jnp.exp(-again))
            D1[...] = sig * (1.0 + again * (1.0 - sig))

        return 0

    lax.fori_loop(0, PARTS + 5 * LOGIT_LAG, logit_tick, 0)

    total = jnp.zeros((16, 1), F32)
    picked = jnp.zeros((16, 1), F32)
    spot = lax.broadcasted_iota(jnp.int32, (16, 128), 0) + z * 16
    lane = lax.broadcasted_iota(jnp.int32, (16, 128), 1)
    target = jnp.sum(jnp.where(spot == lane, tgt[...], 0), axis=1, keepdims=True)
    for p in range(PARTS):
        logits = LF[p]
        hit = lax.broadcasted_iota(jnp.int32, (16, vq), 1) + p * vq == target
        total += jnp.sum(jnp.exp(logits), axis=1, keepdims=True)
        picked += jnp.sum(jnp.where(hit, logits, 0.0), axis=1, keepdims=True)

    def grad_step(p, k):
        for d in (0, 1):
            here = behind(d, k)
            half = slice(d * hc, d * hc + hc)
            if k > 0:
                piece = G.at[p, here, :, half] if k == 4 else G.at[p, here]
                wait(piece, g_r.at[d, p, k - 1])
            if k < 4:
                piece = G.at[p, here, :, half] if k == 3 else G.at[p, here]
                send(piece, piece, g_s.at[k // 3], g_r.at[d, p, k], ring[d])

    def loss_step(k):
        for d in (0, 1):
            here = behind(d, k)
            if k > 0 and (d == 0 or k < 4):
                wait(LT.at[here], lt_r.at[d, k - 1])
            if k < 3 or (k == 3 and d == 0):
                send(LT.at[here], LT.at[here], lt_s, lt_r.at[d, k], ring[d])

    for p in range(PARTS):
        hit = lax.broadcasted_iota(jnp.int32, (16, vq), 1) + p * vq == target
        G[p, z] = (jnp.exp(LF[p]) / total - jnp.where(hit, 1.0, 0.0)).astype(BF16)
        grad_step(p, 0)
    loss = jnp.log(total) - picked
    high = loss.astype(BF16).astype(F32)
    middle = (loss - high).astype(BF16).astype(F32)
    low = loss - high - middle
    LT[z] = jnp.where(
        lane == 0, high, jnp.where(lane == 1, middle, jnp.where(lane == 2, low, 0.0))
    ).astype(BF16)
    loss_step(0)

    def gradient_tick(t, _):
        for k in (3, 2, 1):
            @pl.when(live(t - GRAD_LAG * k, PARTS))
            def _(k=k):
                grad_step(t - GRAD_LAG * k, k)

        @pl.when(live(t - 4 * GRAD_LAG, PARTS))
        def _():
            p = t - 4 * GRAD_LAG
            grad_step(p, 4)
            cols = pl.ds(pl.multiple_of(p * vq, vq), vq)
            part = lax.dot_general(
                G[p].reshape(128, vq), V[:, cols], (((1,), (1,)), ((), ())),
                preferred_element_type=F32,
            )
            DR[...] = jnp.where(p == 0, part, DR[...] + part)

        return 0

    DR[...] = jnp.zeros_like(DR)
    lax.fori_loop(1, PARTS + 4 * GRAD_LAG, gradient_tick, 0)
    DQ[...] = (DR[...] * D1[...]).astype(BF16).reshape(8, 16, units)

    slot = slot_of((x + 4 - shard // 4) % 4, (y_lo + (shard // 2) % 2) % 2)
    for g in range(8):
        device = in_source(g)
        place = DP.at[slot, flip, g]

        @pl.when(is_self(device))
        def _(g=g, place=place):
            pltpu.make_async_copy(DQ.at[g], place, d_r.at[slot]).start()

        @pl.when(jnp.logical_not(is_self(device)))
        def _(g=g, place=place, device=device):
            send(DQ.at[g], place, d_s, d_r.at[slot], device)

    for k in range(1, 5):
        loss_step(k)
    column = jnp.sum(LT[...].reshape(128, 128).astype(F32), axis=1, keepdims=True)
    diagonal = lax.broadcasted_iota(jnp.int32, (128, 128), 0) == lax.broadcasted_iota(jnp.int32, (128, 128), 1)
    loss_out[...] = jnp.sum(jnp.where(diagonal, column, 0.0), axis=0, keepdims=True)

    mt = min(256, units)

    def over_y(piece, r, n):
        send(piece, piece, dy_s.at[n], dy_r.at[r], y_far)

    def even_gather(r, s):
        if s == 5:
            wait(DP.at[r, y_other], dy_r.at[r])
            return
        if s == 0:
            piece = DP.at[r, y_hi, z]
            wait(piece, d_r.at[r])
            for d in (0, 1):
                send(piece, piece, a_s.at[0], a_r.at[d, r, 0], ring[d])
            over_y(piece, r, 0)
            return
        for d in (0, 1):
            here = behind(d, s)
            piece = DP.at[r, y_hi, here]
            half = DP.at[r, y_hi, here, :, d * hu:d * hu + hu]
            if s == 4:
                wait(half, a_r.at[d, r, 3])
                continue
            wait(piece, a_r.at[d, r, s - 1])
            if s == 3:
                send(half, half, a_s.at[1], a_r.at[d, r, 3], ring[d])
            else:
                send(piece, piece, a_s.at[0], a_r.at[d, r, s], ring[d])
            over_y(piece, r, 0)
        if s == 4:
            over_y(DP.at[r, y_hi, behind(0, 4)], r, 0)

    def odd_gather(r, s):
        if s == 0:
            piece = DP.at[r, y_hi, z]
            wait(piece, d_r.at[r])
            over_y(piece, r, 1)
            return
        if s == 1:
            wait(DP.at[r, y_other, z], dy_r.at[r])
        for d in (0, 1):
            here = behind(d, s - 1)
            piece = DP.at[r, :, here]
            half = DP.at[r, d, here]
            if s == 5:
                wait(half, a_r.at[d, r, 3])
                continue
            if s > 1:
                wait(piece, a_r.at[d, r, s - 2])
            if s == 4:
                send(half, half, a_s.at[3], a_r.at[d, r, 3], ring[d])
            else:
                send(piece, piece, a_s.at[2], a_r.at[d, r, s - 1], ring[d])

    def outer(r, m):
        cols = pl.ds(pl.multiple_of(m * mt, mt), mt)
        return lax.dot_general(
            DP[r, :, :, :, cols].reshape(256, mt), H[pl.ds(2 * r, 2)].reshape(256, feats),
            (((0,), (0,)), ((), ())), preferred_element_type=F32,
        )

    def weight_ticks(pair, _):
        for u in (0, 1):
            t = 2 * pair + u
            for s in (4, 3, 2, 1, 0, 5):
                @pl.when(live(t - WEIGHT_LAG * s, ROUNDS))
                def _(s=s, t=t, u=u):
                    (odd_gather if (u - WEIGHT_LAG * s) % 2 else even_gather)(t - WEIGHT_LAG * s, s)

            @pl.when(live(t - 5 * WEIGHT_LAG, ROUNDS - 1))
            def _(t=t):
                def tile(m, _):
                    rows = pl.ds(pl.multiple_of(m * mt, mt), mt)
                    ACC[rows, :] += outer(t - 5 * WEIGHT_LAG, m)
                    return 0

                lax.fori_loop(0, units // mt, tile, 0)

        return 0

    lax.fori_loop(0, (ROUNDS + 5 * WEIGHT_LAG + 1) // 2, weight_ticks, 0)

    def finish(m, _):
        rows = pl.ds(pl.multiple_of(m * mt, mt), mt)
        OUT[rows, :] = (ACC[rows, :] + outer(ROUNDS - 1, m)).astype(BF16)
        pltpu.make_async_copy(OUT.at[rows], out.at[rows], o_s).start()
        return 0

    lax.fori_loop(0, units // mt, finish, 0)

    four = DP.at[0, 0, 0:4]
    eight = DP.at[0, 0]
    wait(H.at[0:15], h_s)
    wait(eight, rs_s.at[0])
    wait(DP.at[0:3], rs_s.at[1])
    wait(four, rs_s.at[2])
    wait(DP.at[0:3, 0], rs_s.at[3])
    wait(four, y_s.at[0])
    wait(DP.at[0:2], y_s.at[1])
    wait(DP.at[0:3, 0], a_s.at[0])
    wait(four, a_s.at[1])
    wait(DP.at[0:3], a_s.at[2])
    wait(eight, a_s.at[3])
    wait(DP.at[0:2], dy_s.at[0])
    wait(four, dy_s.at[1])
    wait(SL, l_s.at[0])
    wait(RL.at[:, 0:3], l_s.at[1])
    wait(LYS, ly_s)
    wait(G.at[0:3], g_s.at[0])
    wait(G.at[0, 0:4], g_s.at[1])
    wait(LT.at[0:7], lt_s)

    for sem, kept in ((m_s, y_hi == 0), (t_s, core == 0), (d_s, own)):
        @pl.when(kept)
        def _(sem=sem):
            wait(DP.at[0, 0, 0:7], sem)

        @pl.when(jnp.logical_not(kept))
        def _(sem=sem):
            wait(eight, sem)

    pltpu.make_async_copy(OUT, out, o_s).wait()


def body(hidden, head_weight, vocab_head, targets):
    feats, units = head_weight.shape
    voc = vocab_head.shape[1]
    vq = voc // PARTS
    pairs = ROUNDS // 2
    dma = pltpu.SemaphoreType.DMA
    one = pltpu.SemaphoreType.DMA
    vmem = pltpu.VMEM
    scratch = [
        vmem((2 * ROUNDS, 128, feats), BF16),
        vmem((feats, units), BF16),
        vmem((units, voc), BF16),
        vmem((ROUNDS, 2, RING, 16, units), F32),
        vmem((2, ROUNDS, 16, units), BF16),
        vmem((2, ROUNDS, 4, 2, 16, units), BF16),
        vmem((pairs, 16, units), BF16),
        vmem((pairs, 16, units), F32),
        vmem((pairs, 16, units), BF16),
        vmem((pairs, RING, 16, units), BF16),
        vmem((pairs, RING, 16, units), BF16),
        vmem((ROUNDS, 16, units), BF16),
        vmem((ROUNDS, 16, units), BF16),
        vmem((8, 16, units), BF16),
        vmem((128, units), BF16),
        vmem((128, units), F32),
        vmem((PARTS, RING, 16, vq), F32),
        vmem((2, PARTS, 16, vq // 2), BF16),
        vmem((2, PARTS, 4, 16, vq), BF16),
        vmem((PARTS, 16, vq), BF16),
        vmem((PARTS, 16, vq), BF16),
        vmem((PARTS, 16, vq), F32),
        vmem((PARTS, RING, 16, vq), BF16),
        vmem((RING, 16, 128), BF16),
        vmem((128, units), F32),
        vmem((8, 16, units), BF16),
        vmem((ROUNDS, 2, RING, 16, units), BF16),
        vmem((units, feats), F32),
        vmem((units, feats), BF16),
        dma((3,)),
        one, dma((2 * ROUNDS,)),
        dma((4,)), dma((2, ROUNDS, 4)),
        dma((2,)), dma((pairs,)), dma((pairs, 5)),
        one, dma((ROUNDS,)),
        one, one,
        dma((2,)), dma((2, PARTS, 4)),
        one, dma((PARTS,)),
        dma((2,)), dma((2, PARTS, 4)),
        one, dma((2, 4)),
        one, dma((ROUNDS,)),
        dma((2,)), dma((ROUNDS,)),
        dma((4,)), dma((2, ROUNDS, 4)),
        one,
    ]
    anywhere = pl.BlockSpec(memory_space=pl.ANY)
    inside = pl.BlockSpec(memory_space=pltpu.VMEM)
    grad, loss = pl.pallas_call(
        kernel,
        out_shape=[
            jax.ShapeDtypeStruct((units, feats), BF16),
            jax.ShapeDtypeStruct((1, 128), F32),
        ],
        in_specs=[anywhere, anywhere, anywhere, inside],
        out_specs=[anywhere, inside],
        scratch_shapes=scratch,
        compiler_params=pltpu.CompilerParams(
            collective_id=0, has_side_effects=True, vmem_limit_bytes=58 * 1024 * 1024
        ),
        name="head",
    )(hidden, head_weight, vocab_head, targets.reshape(1, 128))
    return grad, loss.reshape(targets.shape)


def solution(mesh):
    in_specs = (P("dp", "shard"), P("shard", "dp"), P("shard", None), P("dp"))
    out_specs = (P("dp", "shard"), P("dp"))
    return jax.shard_map(body, mesh=mesh, in_specs=in_specs, out_specs=out_specs, check_vma=False)
```

```python
import jax
import jax.numpy as jnp
from jax import lax
from jax.experimental import pallas as pl
from jax.experimental.pallas import tpu as pltpu
from jax.sharding import PartitionSpec as P

MESH = pl.DeviceIdType.MESH
BF16 = jnp.bfloat16
F32 = jnp.float32

ROUNDS = 8
RING = 8
PARTS = 4
PRE_LAG, LOGIT_LAG, GRAD_LAG, WEIGHT_LAG = 2, 4, 4, 3


def slot_of(dx, a):
    odd = dx % 2
    return odd * (2 + 2 * a + (3 - dx) // 2) + (1 - odd) * (3 * dx + a)


def offset_of(slot):
    middle = jnp.logical_and(slot >= 2, slot <= 5)
    dx = jnp.where(middle, 3 - 2 * (slot % 2), jnp.where(slot >= 6, 2, 0))
    a = jnp.where(middle, (slot // 2 + 1) % 2, slot % 2)
    return dx, a


def send(src, dst, send_sem, recv_sem, device):
    pltpu.make_async_remote_copy(
        src_ref=src,
        dst_ref=dst,
        send_sem=send_sem,
        recv_sem=recv_sem,
        device_id=device,
        device_id_type=MESH,
    ).start()


def wait(ref, sem):
    pltpu.make_async_copy(ref, ref, sem).wait()


def kernel(
    h_in, w_in, v_in, tgt, out, loss_out,
    H, W, V, PT, S0, R, YS, YK, YR, YB, YC, TS, TM, PRE, RES, D1, L, SL, RL, LYS, LYR, LF, G, LT, DR, DQ, DP,
    ACC,
    loc, h_s, h_r, rs_s, rs_r, y_s, y_r, yc_r, m_s, m_r, t_s, t_r, l_s, l_r, ly_s, ly_r, g_s, g_r, lt_s, lt_r,
    d_s, d_r, dy_s, dy_r, a_s, a_r,
):
    dp = lax.axis_index("dp")
    shard = lax.axis_index("shard")
    x, y_lo, core = dp // 4, (dp // 2) % 2, dp % 2
    z, y_hi = shard // 2, shard % 2
    y_other = 1 - y_hi
    feats = H.shape[2]
    units = W.shape[1]
    vq = L.shape[3]
    hu, hc = units // 2, vq // 2

    x_next = ((dp + 4) % 16, shard)
    x_prev = ((dp + 12) % 16, shard)
    y_near = (dp + 2 - 4 * y_lo, shard)
    sibling = (dp + 1 - 2 * core, shard)
    z_next = (dp, (shard + 2) % 16)
    z_prev = (dp, (shard + 14) % 16)
    y_far = (dp, shard + 1 - 2 * y_hi)
    ring = (z_next, z_prev)

    def out_target(slot):
        dx, a = offset_of(slot)
        there = ((x + dx) % 4) * 4 + ((y_lo + a) % 2) * 2 + (core + y_hi) % 2
        return (there, shard)

    def in_column(slot):
        dx, a = offset_of(slot)
        column = ((x + 4 - dx) % 4) * 4 + ((y_lo + a) % 2) * 2 + (core + y_hi) % 2
        return (dp, column)

    flip = (core + shard % 2) % 2

    def in_source(g):
        return (shard, 2 * g + flip)

    def is_self(device):
        return jnp.logical_and(device[0] == dp, device[1] == shard)

    own = jnp.logical_and(dp == shard, y_hi == 0)

    barrier = pltpu.get_barrier_semaphore()
    near = (x_next, x_prev, y_near, sibling, z_next, z_prev, y_far)
    for device in near:
        pl.semaphore_signal(barrier, inc=1, device_id=device, device_id_type=MESH)
    copy_w = pltpu.make_async_copy(w_in, W, loc.at[0])
    copy_w.start()
    copy_h = pltpu.make_async_copy(h_in, H.at[0], loc.at[2])
    copy_h.start()
    copy_v = pltpu.make_async_copy(v_in, V, loc.at[1])
    pl.semaphore_wait(barrier, len(near))

    def pass_on(src, slot, device):
        send(src, H.at[slot], h_s, h_r.at[slot], device)

    pass_on(h_in, 1, sibling)
    pass_on(h_in, 2, y_near)
    pass_on(h_in, 4, x_next)
    pass_on(h_in, 6, x_prev)
    copy_v.start()

    def service(q):
        wait(H.at[2 * q], h_r.at[2 * q])
        pass_on(H.at[2 * q], 2 * q + 1, sibling)

        @pl.when(q == 1)
        def _():
            pass_on(H.at[2], 8, x_next)
            pass_on(H.at[2], 10, x_prev)

        @pl.when(q == 2)
        def _():
            pass_on(H.at[4], 12, x_next)

        @pl.when(q == 5)
        def _():
            pass_on(H.at[10], 14, x_prev)

    copy_h.wait()
    copy_w.wait()

    def ahead(d, k):
        return (z + (RING // 2 - k if d == 0 else RING // 2 + k)) % RING

    def behind(d, k):
        return (z + (RING - k if d == 0 else k)) % RING

    def live(r, n):
        return jnp.logical_and(r >= 0, r < n)

    nt = min(512, units)

    def product(t):
        def tile(n, _):
            cols = pl.ds(pl.multiple_of(n * nt, nt), nt)
            rows = H[pl.ds(2 * t, 2)].reshape(256, feats)
            PT[t, :, :, :, cols] = jnp.dot(
                rows, W[:, cols], preferred_element_type=F32
            ).reshape(2, RING, 16, nt)
            return 0

        lax.fori_loop(0, units // nt, tile, 0)

    def even_step(r, s):
        q = r // 2
        if s == 0:
            for d in (0, 1):
                S0[d, r] = PT[r, d, ahead(d, 0)].astype(BF16)
                send(S0.at[d, r], R.at[d, r, 0, d], rs_s.at[0], rs_r.at[d, r, 0], ring[d])
        elif s < 4:
            for d in (0, 1):
                at = ahead(d, s)
                if s == 1:
                    wait(R.at[d, r, 0, d], rs_r.at[d, r, 0])
                    R[d, r, 0, d] = (PT[r, d, at] + R[d, r, 0, d].astype(F32)).astype(BF16)
                    R[d, r, 0, 1 - d] = PT[r, 1 - d, at].astype(BF16)
                else:
                    wait(R.at[d, r, s - 1], rs_r.at[d, r, s - 1])
                    R[d, r, s - 1] = (PT[r, :, at] + R[d, r, s - 1].astype(F32)).astype(BF16)
                send(R.at[d, r, s - 1], R.at[d, r, s], rs_s.at[1], rs_r.at[d, r, s], ring[d])
        elif s == 4:
            wait(R.at[0, r, 3], rs_r.at[0, r, 3])
            wait(R.at[1, r, 3], rs_r.at[1, r, 3])

            def total(h):
                return PT[r, h, z] + R[0, r, 3, h].astype(F32) + R[1, r, 3, h].astype(F32)

            YS[q] = total(y_other).astype(BF16)
            send(YS.at[q], YR.at[q], y_s.at[0], y_r.at[q], y_far)
            YK[q] = total(y_hi)
        else:
            wait(YR.at[q], y_r.at[q])
            TS[r] = (YK[q] + YR[q].astype(F32)).astype(BF16)

    groups = ((0, 1), (1, 3), (3, 5), (5, 7), (7, 8))

    def odd_step(r, s):
        q = r // 2
        if s == 0:
            for n, (low, high) in enumerate(groups):
                YB[q, low] = PT[r, y_other, ahead(0, n)].astype(BF16)
                if high - low == 2:
                    YB[q, low + 1] = PT[r, y_other, ahead(1, n)].astype(BF16)
                send(YB.at[q, low:high], YC.at[q, low:high], y_s.at[1], yc_r.at[q, n], y_far)
            return
        k = s - 1
        low, high = groups[k]
        wait(YC.at[q, low:high], yc_r.at[q, k])

        def mine(d, cols=slice(None)):
            return PT[r, y_hi, ahead(d, k), :, cols] + YC[q, low if high - low == 1 else low + d, :, cols].astype(F32)

        if k == 4:
            wait(R.at[0, r, 3, 0], rs_r.at[0, r, 3])
            wait(R.at[1, r, 3, 0], rs_r.at[1, r, 3])
            TS[r] = (mine(0) + R[0, r, 3, 0].astype(F32) + R[1, r, 3, 0].astype(F32)).astype(BF16)
            return
        for d in (0, 1):
            half = slice(d * hu, d * hu + hu)
            rest = slice(hu - d * hu, 2 * hu - d * hu)
            if k == 0:
                S0[d, r, :, half] = mine(d, half).astype(BF16)
                send(S0.at[d, r, :, half], R.at[d, r, 0, 0, :, half], rs_s.at[2], rs_r.at[d, r, 0], ring[d])
                continue
            if k == 1:
                wait(R.at[d, r, 0, 0, :, half], rs_r.at[d, r, 0])
                R[d, r, 0, 0, :, half] = (mine(d, half) + R[d, r, 0, 0, :, half].astype(F32)).astype(BF16)
                R[d, r, 0, 0, :, rest] = mine(d, rest).astype(BF16)
            else:
                wait(R.at[d, r, k - 1, 0], rs_r.at[d, r, k - 1])
                R[d, r, k - 1, 0] = (mine(d) + R[d, r, k - 1, 0].astype(F32)).astype(BF16)
            send(R.at[d, r, k - 1, 0], R.at[d, r, k, 0], rs_s.at[3], rs_r.at[d, r, k], ring[d])

    def move(src, dst, send_sem, recv_sem, device):
        @pl.when(is_self(device))
        def _():
            pltpu.make_async_copy(src, dst, recv_sem).start()

        @pl.when(jnp.logical_not(is_self(device)))
        def _():
            send(src, dst, send_sem, recv_sem, device)

    def to_tokens(r):
        move(TS.at[r], TM.at[r], m_s, m_r.at[r], out_target(r))

    def to_features(r):
        wait(TM.at[r], m_r.at[r])
        move(TM.at[r], PRE.at[z], t_s, t_r, in_column(r))

    def pre_ticks(pair, _):
        for u in (0, 1):
            t = 2 * pair + u
            for s in (5, 4, 3, 2, 1):
                @pl.when(live(t - PRE_LAG * s, ROUNDS))
                def _(s=s, t=t, u=u):
                    (odd_step if (u - PRE_LAG * s) % 2 else even_step)(t - PRE_LAG * s, s)
                    if s == 5:
                        to_tokens(t - PRE_LAG * s)

            if u == 1:
                @pl.when(t == 1)
                def _(t=t):
                    service(t)

            @pl.when(t < ROUNDS)
            def _(t=t, u=u):
                wait(H.at[2 * t + 1], h_r.at[2 * t + 1])
                product(t)
                (odd_step if u else even_step)(t, 0)

            @pl.when(jnp.logical_and(t >= 1, t < ROUNDS - 1))
            def _(t=t):
                service(t + 1)

            @pl.when(t == 1)
            def _():
                ACC[...] = jnp.zeros_like(ACC)

            e = t - 5 * (PRE_LAG - 1)

            @pl.when(jnp.logical_and(e >= 9, e <= 11))
            def _(e=e):
                to_features(2 * (e - 9))
                to_features(2 * (e - 9) + 1)

            @pl.when(e == 12)
            def _():
                to_features(6)

        return 0

    lax.fori_loop(0, (ROUNDS + 5 * PRE_LAG + 1) // 2, pre_ticks, 0)

    to_features(7)
    wait(PRE, t_r)
    pre = PRE[...].reshape(128, units).astype(F32)
    RES[...] = (H[0].astype(F32) + pre / (1.0 + jnp.exp(-pre))).astype(BF16)
    copy_v.wait()

    def logit_step(p, k):
        if k == 5:
            wait(LYR.at[p], ly_r.at[p])
            LF[p] = LYS[p].astype(F32) + LYR[p].astype(F32)
            return
        if k == 4:
            wait(RL.at[0, p, 3], l_r.at[0, p, 3])
            wait(RL.at[1, p, 3], l_r.at[1, p, 3])
            LYS[p] = (L[p, z] + RL[0, p, 3].astype(F32) + RL[1, p, 3].astype(F32)).astype(BF16)
            send(LYS.at[p], LYR.at[p], ly_s, ly_r.at[p], y_far)
            return
        for d in (0, 1):
            at = ahead(d, k)
            half = slice(d * hc, d * hc + hc)
            rest = slice(hc - d * hc, 2 * hc - d * hc)
            if k == 0:
                SL[d, p] = L[p, at, :, half].astype(BF16)
                send(SL.at[d, p], RL.at[d, p, 0, :, half], l_s.at[0], l_r.at[d, p, 0], ring[d])
                continue
            if k == 1:
                wait(RL.at[d, p, 0, :, half], l_r.at[d, p, 0])
                RL[d, p, 0, :, half] = (L[p, at, :, half] + RL[d, p, 0, :, half].astype(F32)).astype(BF16)
                RL[d, p, 0, :, rest] = L[p, at, :, rest].astype(BF16)
            else:
                wait(RL.at[d, p, k - 1], l_r.at[d, p, k - 1])
                RL[d, p, k - 1] = (L[p, at] + RL[d, p, k - 1].astype(F32)).astype(BF16)
            send(RL.at[d, p, k - 1], RL.at[d, p, k], l_s.at[1], l_r.at[d, p, k], ring[d])

    def logit_tick(t, _):
        @pl.when(t < PARTS)
        def _():
            cols = pl.ds(pl.multiple_of(t * vq, vq), vq)
            L[t] = jnp.dot(RES[...], V[:, cols], preferred_element_type=F32).reshape(RING, 16, vq)
            logit_step(t, 0)

        for k in (5, 4, 3, 2, 1):
            @pl.when(live(t - LOGIT_LAG * k, PARTS))
            def _(k=k):
                logit_step(t - LOGIT_LAG * k, k)

        @pl.when(t == 4)
        def _():
            again = PRE[...].reshape(128, units).astype(F32)
            sig = 1.0 / (1.0 + jnp.exp(-again))
            D1[...] = sig * (1.0 + again * (1.0 - sig))

        return 0

    lax.fori_loop(0, PARTS + 5 * LOGIT_LAG, logit_tick, 0)

    total = jnp.zeros((16, 1), F32)
    picked = jnp.zeros((16, 1), F32)
    spot = lax.broadcasted_iota(jnp.int32, (16, 128), 0) + z * 16
    lane = lax.broadcasted_iota(jnp.int32, (16, 128), 1)
    target = jnp.sum(jnp.where(spot == lane, tgt[...], 0), axis=1, keepdims=True)
    for p in range(PARTS):
        logits = LF[p]
        hit = lax.broadcasted_iota(jnp.int32, (16, vq), 1) + p * vq == target
        total += jnp.sum(jnp.exp(logits), axis=1, keepdims=True)
        picked += jnp.sum(jnp.where(hit, logits, 0.0), axis=1, keepdims=True)

    def grad_step(p, k):
        for d in (0, 1):
            here = behind(d, k)
            half = slice(d * hc, d * hc + hc)
            if k > 0:
                piece = G.at[p, here, :, half] if k == 4 else G.at[p, here]
                wait(piece, g_r.at[d, p, k - 1])
            if k < 4:
                piece = G.at[p, here, :, half] if k == 3 else G.at[p, here]
                send(piece, piece, g_s.at[k // 3], g_r.at[d, p, k], ring[d])

    def loss_step(k):
        for d in (0, 1):
            here = behind(d, k)
            if k > 0 and (d == 0 or k < 4):
                wait(LT.at[here], lt_r.at[d, k - 1])
            if k < 3 or (k == 3 and d == 0):
                send(LT.at[here], LT.at[here], lt_s, lt_r.at[d, k], ring[d])

    for p in range(PARTS):
        hit = lax.broadcasted_iota(jnp.int32, (16, vq), 1) + p * vq == target
        G[p, z] = (jnp.exp(LF[p]) / total - jnp.where(hit, 1.0, 0.0)).astype(BF16)
        grad_step(p, 0)
    loss = jnp.log(total) - picked
    high = loss.astype(BF16).astype(F32)
    middle = (loss - high).astype(BF16).astype(F32)
    low = loss - high - middle
    LT[z] = jnp.where(
        lane == 0, high, jnp.where(lane == 1, middle, jnp.where(lane == 2, low, 0.0))
    ).astype(BF16)
    loss_step(0)

    def gradient_tick(t, _):
        for k in (3, 2, 1):
            @pl.when(live(t - GRAD_LAG * k, PARTS))
            def _(k=k):
                grad_step(t - GRAD_LAG * k, k)

        @pl.when(live(t - 4 * GRAD_LAG, PARTS))
        def _():
            p = t - 4 * GRAD_LAG
            grad_step(p, 4)
            cols = pl.ds(pl.multiple_of(p * vq, vq), vq)
            part = lax.dot_general(
                G[p].reshape(128, vq), V[:, cols], (((1,), (1,)), ((), ())),
                preferred_element_type=F32,
            )
            DR[...] = jnp.where(p == 0, part, DR[...] + part)

        for k in (1, 2, 3, 4):
            @pl.when(t == GRAD_LAG * k)
            def _(k=k):
                loss_step(k)

        return 0

    DR[...] = jnp.zeros_like(DR)
    lax.fori_loop(1, PARTS + 4 * GRAD_LAG, gradient_tick, 0)
    DQ[...] = (DR[...] * D1[...]).astype(BF16).reshape(8, 16, units)

    slot = slot_of((x + 4 - shard // 4) % 4, (y_lo + (shard // 2) % 2) % 2)
    for g in range(8):
        device = in_source(g)
        place = DP.at[slot, flip, g]

        @pl.when(is_self(device))
        def _(g=g, place=place):
            pltpu.make_async_copy(DQ.at[g], place, d_r.at[slot]).start()

        @pl.when(jnp.logical_not(is_self(device)))
        def _(g=g, place=place, device=device):
            send(DQ.at[g], place, d_s, d_r.at[slot], device)

    column = jnp.sum(LT[...].reshape(128, 128).astype(F32), axis=1, keepdims=True)
    diagonal = lax.broadcasted_iota(jnp.int32, (128, 128), 0) == lax.broadcasted_iota(jnp.int32, (128, 128), 1)
    loss_out[...] = jnp.sum(jnp.where(diagonal, column, 0.0), axis=0, keepdims=True)

    mt = min(256, units)

    def over_y(piece, r, n):
        send(piece, piece, dy_s.at[n], dy_r.at[r], y_far)

    def even_gather(r, s):
        if s == 5:
            wait(DP.at[r, y_other], dy_r.at[r])
            return
        if s == 0:
            piece = DP.at[r, y_hi, z]
            wait(piece, d_r.at[r])
            for d in (0, 1):
                send(piece, piece, a_s.at[0], a_r.at[d, r, 0], ring[d])
            over_y(piece, r, 0)
            return
        for d in (0, 1):
            here = behind(d, s)
            piece = DP.at[r, y_hi, here]
            half = DP.at[r, y_hi, here, :, d * hu:d * hu + hu]
            if s == 4:
                wait(half, a_r.at[d, r, 3])
                continue
            wait(piece, a_r.at[d, r, s - 1])
            if s == 3:
                send(half, half, a_s.at[1], a_r.at[d, r, 3], ring[d])
            else:
                send(piece, piece, a_s.at[0], a_r.at[d, r, s], ring[d])
            over_y(piece, r, 0)
        if s == 4:
            over_y(DP.at[r, y_hi, behind(0, 4)], r, 0)

    def odd_gather(r, s):
        if s == 0:
            piece = DP.at[r, y_hi, z]
            wait(piece, d_r.at[r])
            over_y(piece, r, 1)
            return
        if s == 1:
            wait(DP.at[r, y_other, z], dy_r.at[r])
        for d in (0, 1):
            here = behind(d, s - 1)
            piece = DP.at[r, :, here]
            half = DP.at[r, d, here]
            if s == 5:
                wait(half, a_r.at[d, r, 3])
                continue
            if s > 1:
                wait(piece, a_r.at[d, r, s - 2])
            if s == 4:
                send(half, half, a_s.at[3], a_r.at[d, r, 3], ring[d])
            else:
                send(piece, piece, a_s.at[2], a_r.at[d, r, s - 1], ring[d])

    def outer(r, m):
        cols = pl.ds(pl.multiple_of(m * mt, mt), mt)
        return lax.dot_general(
            DP[r, :, :, :, cols].reshape(256, mt), H[pl.ds(2 * r, 2)].reshape(256, feats),
            (((0,), (0,)), ((), ())), preferred_element_type=F32,
        )

    def weight_ticks(pair, _):
        for u in (0, 1):
            t = 2 * pair + u
            for s in (4, 3, 2, 1, 0, 5):
                @pl.when(live(t - WEIGHT_LAG * s, ROUNDS))
                def _(s=s, t=t, u=u):
                    (odd_gather if (u - WEIGHT_LAG * s) % 2 else even_gather)(t - WEIGHT_LAG * s, s)

            @pl.when(live(t - 5 * WEIGHT_LAG, ROUNDS - 1))
            def _(t=t):
                def tile(m, _):
                    rows = pl.ds(pl.multiple_of(m * mt, mt), mt)
                    ACC[rows, :] += outer(t - 5 * WEIGHT_LAG, m)
                    return 0

                lax.fori_loop(0, units // mt, tile, 0)

        return 0

    lax.fori_loop(0, (ROUNDS + 5 * WEIGHT_LAG + 1) // 2, weight_ticks, 0)

    def finish(m, _):
        rows = pl.ds(pl.multiple_of(m * mt, mt), mt)
        out[rows, :] = (ACC[rows, :] + outer(ROUNDS - 1, m)).astype(BF16)
        return 0

    lax.fori_loop(0, units // mt, finish, 0)

    four = DP.at[0, 0, 0:4]
    eight = DP.at[0, 0]
    wait(H.at[0:15], h_s)
    wait(eight, rs_s.at[0])
    wait(DP.at[0:3], rs_s.at[1])
    wait(four, rs_s.at[2])
    wait(DP.at[0:3, 0], rs_s.at[3])
    wait(four, y_s.at[0])
    wait(DP.at[0:2], y_s.at[1])
    wait(DP.at[0:3, 0], a_s.at[0])
    wait(four, a_s.at[1])
    wait(DP.at[0:3], a_s.at[2])
    wait(eight, a_s.at[3])
    wait(DP.at[0:2], dy_s.at[0])
    wait(four, dy_s.at[1])
    wait(SL, l_s.at[0])
    wait(RL.at[:, 0:3], l_s.at[1])
    wait(LYS, ly_s)
    wait(G.at[0:3], g_s.at[0])
    wait(G.at[0, 0:4], g_s.at[1])
    wait(LT.at[0:7], lt_s)

    for sem, kept in ((m_s, y_hi == 0), (t_s, core == 0), (d_s, own)):
        @pl.when(kept)
        def _(sem=sem):
            wait(DP.at[0, 0, 0:7], sem)

        @pl.when(jnp.logical_not(kept))
        def _(sem=sem):
            wait(eight, sem)


def body(hidden, head_weight, vocab_head, targets):
    feats, units = head_weight.shape
    voc = vocab_head.shape[1]
    vq = voc // PARTS
    pairs = ROUNDS // 2
    dma = pltpu.SemaphoreType.DMA
    one = pltpu.SemaphoreType.DMA
    vmem = pltpu.VMEM
    scratch = [
        vmem((2 * ROUNDS, 128, feats), BF16),
        vmem((feats, units), BF16),
        vmem((units, voc), BF16),
        vmem((ROUNDS, 2, RING, 16, units), F32),
        vmem((2, ROUNDS, 16, units), BF16),
        vmem((2, ROUNDS, 4, 2, 16, units), BF16),
        vmem((pairs, 16, units), BF16),
        vmem((pairs, 16, units), F32),
        vmem((pairs, 16, units), BF16),
        vmem((pairs, RING, 16, units), BF16),
        vmem((pairs, RING, 16, units), BF16),
        vmem((ROUNDS, 16, units), BF16),
        vmem((ROUNDS, 16, units), BF16),
        vmem((8, 16, units), BF16),
        vmem((128, units), BF16),
        vmem((128, units), F32),
        vmem((PARTS, RING, 16, vq), F32),
        vmem((2, PARTS, 16, vq // 2), BF16),
        vmem((2, PARTS, 4, 16, vq), BF16),
        vmem((PARTS, 16, vq), BF16),
        vmem((PARTS, 16, vq), BF16),
        vmem((PARTS, 16, vq), F32),
        vmem((PARTS, RING, 16, vq), BF16),
        vmem((RING, 16, 128), BF16),
        vmem((128, units), F32),
        vmem((8, 16, units), BF16),
        vmem((ROUNDS, 2, RING, 16, units), BF16),
        vmem((units, feats), F32),
        dma((3,)),
        one, dma((2 * ROUNDS,)),
        dma((4,)), dma((2, ROUNDS, 4)),
        dma((2,)), dma((pairs,)), dma((pairs, 5)),
        one, dma((ROUNDS,)),
        one, one,
        dma((2,)), dma((2, PARTS, 4)),
        one, dma((PARTS,)),
        dma((2,)), dma((2, PARTS, 4)),
        one, dma((2, 4)),
        one, dma((ROUNDS,)),
        dma((2,)), dma((ROUNDS,)),
        dma((4,)), dma((2, ROUNDS, 4)),
    ]
    anywhere = pl.BlockSpec(memory_space=pl.ANY)
    inside = pl.BlockSpec(memory_space=pltpu.VMEM)
    grad, loss = pl.pallas_call(
        kernel,
        out_shape=[
            pltpu.VMEM((units, feats), BF16),
            jax.ShapeDtypeStruct((1, 128), F32),
        ],
        in_specs=[anywhere, anywhere, anywhere, inside],
        out_specs=[inside, inside],
        scratch_shapes=scratch,
        compiler_params=pltpu.CompilerParams(
            collective_id=0, has_side_effects=True, vmem_limit_bytes=56 * 1024 * 1024
        ),
        name="head",
    )(hidden, head_weight, vocab_head, targets.reshape(1, 128))
    return grad, loss.reshape(targets.shape)


def solution(mesh):
    in_specs = (P("dp", "shard"), P("shard", "dp"), P("shard", None), P("dp"))
    out_specs = (P("dp", "shard"), P("dp"))
    return jax.shard_map(body, mesh=mesh, in_specs=in_specs, out_specs=out_specs, check_vma=False)
```

```python
import jax
import jax.numpy as jnp
from jax import lax
from jax.experimental import pallas as pl
from jax.experimental.pallas import tpu as pltpu
from jax.sharding import PartitionSpec as P

MESH = pl.DeviceIdType.MESH
BF16 = jnp.bfloat16
F32 = jnp.float32

ROUNDS = 8
RING = 8
PARTS = 4
PRE_LAG, LOGIT_LAG, GRAD_LAG, WEIGHT_LAG = 2, 4, 4, 3


def slot_of(dx, a):
    odd = dx % 2
    return odd * (2 + 2 * a + (3 - dx) // 2) + (1 - odd) * (3 * dx + a)


def offset_of(slot):
    middle = jnp.logical_and(slot >= 2, slot <= 5)
    dx = jnp.where(middle, 3 - 2 * (slot % 2), jnp.where(slot >= 6, 2, 0))
    a = jnp.where(middle, (slot // 2 + 1) % 2, slot % 2)
    return dx, a


def send(src, dst, send_sem, recv_sem, device):
    pltpu.make_async_remote_copy(
        src_ref=src,
        dst_ref=dst,
        send_sem=send_sem,
        recv_sem=recv_sem,
        device_id=device,
        device_id_type=MESH,
    ).start()


def wait(ref, sem):
    pltpu.make_async_copy(ref, ref, sem).wait()


def kernel(
    h_in, w_in, v_in, tgt, out, loss_out,
    H, W, V, PT, S0, R, YS, YK, YR, YB, YC, TS, TM, PRE, RES, D1, L, SL, RL, LYS, LYR, LF, G, LT, DR, DQ, DP,
    ACC,
    loc, h_s, h_r, rs_s, rs_r, y_s, y_r, yc_r, m_s, m_r, t_s, t_r, l_s, l_r, ly_s, ly_r, g_s, g_r, lt_s, lt_r,
    d_s, d_r, dy_s, dy_r, a_s, a_r,
):
    dp = lax.axis_index("dp")
    shard = lax.axis_index("shard")
    x, y_lo, core = dp // 4, (dp // 2) % 2, dp % 2
    z, y_hi = shard // 2, shard % 2
    y_other = 1 - y_hi
    feats = H.shape[2]
    units = W.shape[1]
    vq = L.shape[3]
    hu, hc = units // 2, vq // 2

    x_next = ((dp + 4) % 16, shard)
    x_prev = ((dp + 12) % 16, shard)
    y_near = (dp + 2 - 4 * y_lo, shard)
    sibling = (dp + 1 - 2 * core, shard)
    z_next = (dp, (shard + 2) % 16)
    z_prev = (dp, (shard + 14) % 16)
    y_far = (dp, shard + 1 - 2 * y_hi)
    ring = (z_next, z_prev)

    def out_target(slot):
        dx, a = offset_of(slot)
        there = ((x + dx) % 4) * 4 + ((y_lo + a) % 2) * 2 + (core + y_hi) % 2
        return (there, shard)

    def in_column(slot):
        dx, a = offset_of(slot)
        column = ((x + 4 - dx) % 4) * 4 + ((y_lo + a) % 2) * 2 + (core + y_hi) % 2
        return (dp, column)

    flip = (core + shard % 2) % 2

    def in_source(g):
        return (shard, 2 * g + flip)

    def is_self(device):
        return jnp.logical_and(device[0] == dp, device[1] == shard)

    own = jnp.logical_and(dp == shard, y_hi == 0)

    barrier = pltpu.get_barrier_semaphore()
    near = (x_next, x_prev, y_near, sibling, z_next, z_prev, y_far)
    for device in near:
        pl.semaphore_signal(barrier, inc=1, device_id=device, device_id_type=MESH)
    copy_w = pltpu.make_async_copy(w_in, W, loc.at[0])
    copy_w.start()
    copy_h = pltpu.make_async_copy(h_in, H.at[0], loc.at[2])
    copy_h.start()
    copy_v = pltpu.make_async_copy(v_in, V, loc.at[1])
    pl.semaphore_wait(barrier, len(near))

    def pass_on(src, slot, device):
        send(src, H.at[slot], h_s, h_r.at[slot], device)

    pass_on(h_in, 1, sibling)
    pass_on(h_in, 2, y_near)
    pass_on(h_in, 4, x_next)
    pass_on(h_in, 6, x_prev)
    copy_v.start()

    def service(q):
        wait(H.at[2 * q], h_r.at[2 * q])
        pass_on(H.at[2 * q], 2 * q + 1, sibling)

        @pl.when(q == 1)
        def _():
            pass_on(H.at[2], 8, x_next)
            pass_on(H.at[2], 10, x_prev)

        @pl.when(q == 2)
        def _():
            pass_on(H.at[4], 12, x_next)

        @pl.when(q == 5)
        def _():
            pass_on(H.at[10], 14, x_prev)

    copy_h.wait()
    copy_w.wait()

    def ahead(d, k):
        return (z + (RING // 2 - k if d == 0 else RING // 2 + k)) % RING

    def behind(d, k):
        return (z + (RING - k if d == 0 else k)) % RING

    def live(r, n):
        return jnp.logical_and(r >= 0, r < n)

    nt = min(512, units)

    def product(t):
        def tile(n, _):
            cols = pl.ds(pl.multiple_of(n * nt, nt), nt)
            rows = H[pl.ds(2 * t, 2)].reshape(256, feats)
            PT[t, :, :, :, cols] = jnp.dot(
                rows, W[:, cols], preferred_element_type=F32
            ).reshape(2, RING, 16, nt)
            return 0

        lax.fori_loop(0, units // nt, tile, 0)

    def first_product(b):
        def tile(n, _):
            cols = pl.ds(pl.multiple_of(n * nt, nt), nt)
            PT[0, b, :, :, cols] = jnp.dot(
                H[b], W[:, cols], preferred_element_type=F32
            ).reshape(RING, 16, nt)
            return 0

        lax.fori_loop(0, units // nt, tile, 0)

    first_product(0)

    def even_step(r, s):
        q = r // 2
        if s == 0:
            for d in (0, 1):
                S0[d, r] = PT[r, d, ahead(d, 0)].astype(BF16)
                send(S0.at[d, r], R.at[d, r, 0, d], rs_s.at[0], rs_r.at[d, r, 0], ring[d])
        elif s < 4:
            for d in (0, 1):
                at = ahead(d, s)
                if s == 1:
                    wait(R.at[d, r, 0, d], rs_r.at[d, r, 0])
                    R[d, r, 0, d] = (PT[r, d, at] + R[d, r, 0, d].astype(F32)).astype(BF16)
                    R[d, r, 0, 1 - d] = PT[r, 1 - d, at].astype(BF16)
                else:
                    wait(R.at[d, r, s - 1], rs_r.at[d, r, s - 1])
                    R[d, r, s - 1] = (PT[r, :, at] + R[d, r, s - 1].astype(F32)).astype(BF16)
                send(R.at[d, r, s - 1], R.at[d, r, s], rs_s.at[1], rs_r.at[d, r, s], ring[d])
        elif s == 4:
            wait(R.at[0, r, 3], rs_r.at[0, r, 3])
            wait(R.at[1, r, 3], rs_r.at[1, r, 3])

            def total(h):
                return PT[r, h, z] + R[0, r, 3, h].astype(F32) + R[1, r, 3, h].astype(F32)

            YS[q] = total(y_other).astype(BF16)
            send(YS.at[q], YR.at[q], y_s.at[0], y_r.at[q], y_far)
            YK[q] = total(y_hi)
        else:
            wait(YR.at[q], y_r.at[q])
            TS[r] = (YK[q] + YR[q].astype(F32)).astype(BF16)

    groups = ((0, 1), (1, 3), (3, 5), (5, 7), (7, 8))

    def odd_step(r, s):
        q = r // 2
        if s == 0:
            for n, (low, high) in enumerate(groups):
                YB[q, low] = PT[r, y_other, ahead(0, n)].astype(BF16)
                if high - low == 2:
                    YB[q, low + 1] = PT[r, y_other, ahead(1, n)].astype(BF16)
                send(YB.at[q, low:high], YC.at[q, low:high], y_s.at[1], yc_r.at[q, n], y_far)
            return
        k = s - 1
        low, high = groups[k]
        wait(YC.at[q, low:high], yc_r.at[q, k])

        def mine(d, cols=slice(None)):
            return PT[r, y_hi, ahead(d, k), :, cols] + YC[q, low if high - low == 1 else low + d, :, cols].astype(F32)

        if k == 4:
            wait(R.at[0, r, 3, 0], rs_r.at[0, r, 3])
            wait(R.at[1, r, 3, 0], rs_r.at[1, r, 3])
            TS[r] = (mine(0) + R[0, r, 3, 0].astype(F32) + R[1, r, 3, 0].astype(F32)).astype(BF16)
            return
        for d in (0, 1):
            half = slice(d * hu, d * hu + hu)
            rest = slice(hu - d * hu, 2 * hu - d * hu)
            if k == 0:
                S0[d, r, :, half] = mine(d, half).astype(BF16)
                send(S0.at[d, r, :, half], R.at[d, r, 0, 0, :, half], rs_s.at[2], rs_r.at[d, r, 0], ring[d])
                continue
            if k == 1:
                wait(R.at[d, r, 0, 0, :, half], rs_r.at[d, r, 0])
                R[d, r, 0, 0, :, half] = (mine(d, half) + R[d, r, 0, 0, :, half].astype(F32)).astype(BF16)
                R[d, r, 0, 0, :, rest] = mine(d, rest).astype(BF16)
            else:
                wait(R.at[d, r, k - 1, 0], rs_r.at[d, r, k - 1])
                R[d, r, k - 1, 0] = (mine(d) + R[d, r, k - 1, 0].astype(F32)).astype(BF16)
            send(R.at[d, r, k - 1, 0], R.at[d, r, k, 0], rs_s.at[3], rs_r.at[d, r, k], ring[d])

    def move(src, dst, send_sem, recv_sem, device):
        @pl.when(is_self(device))
        def _():
            pltpu.make_async_copy(src, dst, recv_sem).start()

        @pl.when(jnp.logical_not(is_self(device)))
        def _():
            send(src, dst, send_sem, recv_sem, device)

    def to_tokens(r):
        move(TS.at[r], TM.at[r], m_s, m_r.at[r], out_target(r))

    def to_features(r):
        wait(TM.at[r], m_r.at[r])
        move(TM.at[r], PRE.at[z], t_s, t_r, in_column(r))

    def pre_ticks(pair, _):
        for u in (0, 1):
            t = 2 * pair + u
            for s in (5, 4, 3, 2, 1):
                @pl.when(live(t - PRE_LAG * s, ROUNDS))
                def _(s=s, t=t, u=u):
                    (odd_step if (u - PRE_LAG * s) % 2 else even_step)(t - PRE_LAG * s, s)
                    if s == 5:
                        to_tokens(t - PRE_LAG * s)

            if u == 1:
                @pl.when(t == 1)
                def _(t=t):
                    service(t)

            @pl.when(t < ROUNDS)
            def _(t=t, u=u):
                wait(H.at[2 * t + 1], h_r.at[2 * t + 1])
                if u:
                    product(t)
                else:
                    @pl.when(t == 0)
                    def _():
                        first_product(1)

                    @pl.when(t > 0)
                    def _():
                        product(t)

                (odd_step if u else even_step)(t, 0)

            @pl.when(jnp.logical_and(t >= 1, t < ROUNDS - 1))
            def _(t=t):
                service(t + 1)

            @pl.when(t == 1)
            def _():
                ACC[...] = jnp.zeros_like(ACC)

            e = t - 5 * (PRE_LAG - 1)

            @pl.when(jnp.logical_and(e >= 9, e <= 11))
            def _(e=e):
                to_features(2 * (e - 9))
                to_features(2 * (e - 9) + 1)

            @pl.when(e == 12)
            def _():
                to_features(6)

        return 0

    lax.fori_loop(0, (ROUNDS + 5 * PRE_LAG + 1) // 2, pre_ticks, 0)

    to_features(7)
    wait(PRE, t_r)
    pre = PRE[...].reshape(128, units).astype(F32)
    RES[...] = (H[0].astype(F32) + pre / (1.0 + jnp.exp(-pre))).astype(BF16)
    copy_v.wait()

    def logit_step(p, k):
        if k == 5:
            wait(LYR.at[p], ly_r.at[p])
            LF[p] = LYS[p].astype(F32) + LYR[p].astype(F32)
            return
        if k == 4:
            wait(RL.at[0, p, 3], l_r.at[0, p, 3])
            wait(RL.at[1, p, 3], l_r.at[1, p, 3])
            LYS[p] = (L[p, z] + RL[0, p, 3].astype(F32) + RL[1, p, 3].astype(F32)).astype(BF16)
            send(LYS.at[p], LYR.at[p], ly_s, ly_r.at[p], y_far)
            return
        for d in (0, 1):
            at = ahead(d, k)
            half = slice(d * hc, d * hc + hc)
            rest = slice(hc - d * hc, 2 * hc - d * hc)
            if k == 0:
                SL[d, p] = L[p, at, :, half].astype(BF16)
                send(SL.at[d, p], RL.at[d, p, 0, :, half], l_s.at[0], l_r.at[d, p, 0], ring[d])
                continue
            if k == 1:
                wait(RL.at[d, p, 0, :, half], l_r.at[d, p, 0])
                RL[d, p, 0, :, half] = (L[p, at, :, half] + RL[d, p, 0, :, half].astype(F32)).astype(BF16)
                RL[d, p, 0, :, rest] = L[p, at, :, rest].astype(BF16)
            else:
                wait(RL.at[d, p, k - 1], l_r.at[d, p, k - 1])
                RL[d, p, k - 1] = (L[p, at] + RL[d, p, k - 1].astype(F32)).astype(BF16)
            send(RL.at[d, p, k - 1], RL.at[d, p, k], l_s.at[1], l_r.at[d, p, k], ring[d])

    def logit_tick(t, _):
        @pl.when(t < PARTS)
        def _():
            cols = pl.ds(pl.multiple_of(t * vq, vq), vq)
            L[t] = jnp.dot(RES[...], V[:, cols], preferred_element_type=F32).reshape(RING, 16, vq)
            logit_step(t, 0)

        for k in (5, 4, 3, 2, 1):
            @pl.when(live(t - LOGIT_LAG * k, PARTS))
            def _(k=k):
                logit_step(t - LOGIT_LAG * k, k)

        @pl.when(t == 4)
        def _():
            again = PRE[...].reshape(128, units).astype(F32)
            sig = 1.0 / (1.0 + jnp.exp(-again))
            D1[...] = sig * (1.0 + again * (1.0 - sig))

        return 0

    lax.fori_loop(0, PARTS + 5 * LOGIT_LAG, logit_tick, 0)

    total = jnp.zeros((16, 1), F32)
    picked = jnp.zeros((16, 1), F32)
    spot = lax.broadcasted_iota(jnp.int32, (16, 128), 0) + z * 16
    lane = lax.broadcasted_iota(jnp.int32, (16, 128), 1)
    target = jnp.sum(jnp.where(spot == lane, tgt[...], 0), axis=1, keepdims=True)
    for p in range(PARTS):
        logits = LF[p]
        hit = lax.broadcasted_iota(jnp.int32, (16, vq), 1) + p * vq == target
        total += jnp.sum(jnp.exp(logits), axis=1, keepdims=True)
        picked += jnp.sum(jnp.where(hit, logits, 0.0), axis=1, keepdims=True)

    def grad_step(p, k):
        for d in (0, 1):
            here = behind(d, k)
            half = slice(d * hc, d * hc + hc)
            if k > 0:
                piece = G.at[p, here, :, half] if k == 4 else G.at[p, here]
                wait(piece, g_r.at[d, p, k - 1])
            if k < 4:
                piece = G.at[p, here, :, half] if k == 3 else G.at[p, here]
                send(piece, piece, g_s.at[k // 3], g_r.at[d, p, k], ring[d])

    def loss_step(k):
        for d in (0, 1):
            here = behind(d, k)
            if k > 0 and (d == 0 or k < 4):
                wait(LT.at[here], lt_r.at[d, k - 1])
            if k < 3 or (k == 3 and d == 0):
                send(LT.at[here], LT.at[here], lt_s, lt_r.at[d, k], ring[d])

    for p in range(PARTS):
        hit = lax.broadcasted_iota(jnp.int32, (16, vq), 1) + p * vq == target
        G[p, z] = (jnp.exp(LF[p]) / total - jnp.where(hit, 1.0, 0.0)).astype(BF16)
        grad_step(p, 0)
    loss = jnp.log(total) - picked
    high = loss.astype(BF16).astype(F32)
    middle = (loss - high).astype(BF16).astype(F32)
    low = loss - high - middle
    LT[z] = jnp.where(
        lane == 0, high, jnp.where(lane == 1, middle, jnp.where(lane == 2, low, 0.0))
    ).astype(BF16)
    loss_step(0)

    def gradient_tick(t, _):
        for k in (3, 2, 1):
            @pl.when(live(t - GRAD_LAG * k, PARTS))
            def _(k=k):
                grad_step(t - GRAD_LAG * k, k)

        @pl.when(live(t - 4 * GRAD_LAG, PARTS))
        def _():
            p = t - 4 * GRAD_LAG
            grad_step(p, 4)
            cols = pl.ds(pl.multiple_of(p * vq, vq), vq)
            part = lax.dot_general(
                G[p].reshape(128, vq), V[:, cols], (((1,), (1,)), ((), ())),
                preferred_element_type=F32,
            )
            DR[...] = jnp.where(p == 0, part, DR[...] + part)

        for k in (1, 2, 3, 4):
            @pl.when(t == GRAD_LAG * k)
            def _(k=k):
                loss_step(k)

        return 0

    DR[...] = jnp.zeros_like(DR)
    lax.fori_loop(1, PARTS + 4 * GRAD_LAG, gradient_tick, 0)
    DQ[...] = (DR[...] * D1[...]).astype(BF16).reshape(8, 16, units)

    slot = slot_of((x + 4 - shard // 4) % 4, (y_lo + (shard // 2) % 2) % 2)
    for g in range(8):
        device = in_source(g)
        place = DP.at[slot, flip, g]

        @pl.when(is_self(device))
        def _(g=g, place=place):
            pltpu.make_async_copy(DQ.at[g], place, d_r.at[slot]).start()

        @pl.when(jnp.logical_not(is_self(device)))
        def _(g=g, place=place, device=device):
            send(DQ.at[g], place, d_s, d_r.at[slot], device)

    column = jnp.sum(LT[...].reshape(128, 128).astype(F32), axis=1, keepdims=True)
    diagonal = lax.broadcasted_iota(jnp.int32, (128, 128), 0) == lax.broadcasted_iota(jnp.int32, (128, 128), 1)
    loss_out[...] = jnp.sum(jnp.where(diagonal, column, 0.0), axis=0, keepdims=True)

    mt = min(256, units)

    def over_y(piece, r, n):
        send(piece, piece, dy_s.at[n], dy_r.at[r], y_far)

    def even_gather(r, s):
        if s == 5:
            wait(DP.at[r, y_other], dy_r.at[r])
            return
        if s == 0:
            piece = DP.at[r, y_hi, z]
            wait(piece, d_r.at[r])
            for d in (0, 1):
                send(piece, piece, a_s.at[0], a_r.at[d, r, 0], ring[d])
            over_y(piece, r, 0)
            return
        for d in (0, 1):
            here = behind(d, s)
            piece = DP.at[r, y_hi, here]
            half = DP.at[r, y_hi, here, :, d * hu:d * hu + hu]
            if s == 4:
                wait(half, a_r.at[d, r, 3])
                continue
            wait(piece, a_r.at[d, r, s - 1])
            if s == 3:
                send(half, half, a_s.at[1], a_r.at[d, r, 3], ring[d])
            else:
                send(piece, piece, a_s.at[0], a_r.at[d, r, s], ring[d])
            over_y(piece, r, 0)
        if s == 4:
            over_y(DP.at[r, y_hi, behind(0, 4)], r, 0)

    def odd_gather(r, s):
        if s == 0:
            piece = DP.at[r, y_hi, z]
            wait(piece, d_r.at[r])
            over_y(piece, r, 1)
            return
        if s == 1:
            wait(DP.at[r, y_other, z], dy_r.at[r])
        for d in (0, 1):
            here = behind(d, s - 1)
            piece = DP.at[r, :, here]
            half = DP.at[r, d, here]
            if s == 5:
                wait(half, a_r.at[d, r, 3])
                continue
            if s > 1:
                wait(piece, a_r.at[d, r, s - 2])
            if s == 4:
                send(half, half, a_s.at[3], a_r.at[d, r, 3], ring[d])
            else:
                send(piece, piece, a_s.at[2], a_r.at[d, r, s - 1], ring[d])

    def outer(r, m):
        cols = pl.ds(pl.multiple_of(m * mt, mt), mt)
        return lax.dot_general(
            DP[r, :, :, :, cols].reshape(256, mt), H[pl.ds(2 * r, 2)].reshape(256, feats),
            (((0,), (0,)), ((), ())), preferred_element_type=F32,
        )

    def weight_ticks(pair, _):
        for u in (0, 1):
            t = 2 * pair + u
            for s in (4, 3, 2, 1, 0, 5):
                @pl.when(live(t - WEIGHT_LAG * s, ROUNDS))
                def _(s=s, t=t, u=u):
                    (odd_gather if (u - WEIGHT_LAG * s) % 2 else even_gather)(t - WEIGHT_LAG * s, s)

            @pl.when(live(t - 5 * WEIGHT_LAG, ROUNDS - 1))
            def _(t=t):
                def tile(m, _):
                    rows = pl.ds(pl.multiple_of(m * mt, mt), mt)
                    ACC[rows, :] += outer(t - 5 * WEIGHT_LAG, m)
                    return 0

                lax.fori_loop(0, units // mt, tile, 0)

        return 0

    lax.fori_loop(0, (ROUNDS + 5 * WEIGHT_LAG + 1) // 2, weight_ticks, 0)

    def finish(m, _):
        rows = pl.ds(pl.multiple_of(m * mt, mt), mt)
        out[rows, :] = (ACC[rows, :] + outer(ROUNDS - 1, m)).astype(BF16)
        return 0

    lax.fori_loop(0, units // mt, finish, 0)

    four = DP.at[0, 0, 0:4]
    eight = DP.at[0, 0]
    wait(H.at[0:15], h_s)
    wait(eight, rs_s.at[0])
    wait(DP.at[0:3], rs_s.at[1])
    wait(four, rs_s.at[2])
    wait(DP.at[0:3, 0], rs_s.at[3])
    wait(four, y_s.at[0])
    wait(DP.at[0:2], y_s.at[1])
    wait(DP.at[0:3, 0], a_s.at[0])
    wait(four, a_s.at[1])
    wait(DP.at[0:3], a_s.at[2])
    wait(eight, a_s.at[3])
    wait(DP.at[0:2], dy_s.at[0])
    wait(four, dy_s.at[1])
    wait(SL, l_s.at[0])
    wait(RL.at[:, 0:3], l_s.at[1])
    wait(LYS, ly_s)
    wait(G.at[0:3], g_s.at[0])
    wait(G.at[0, 0:4], g_s.at[1])
    wait(LT.at[0:7], lt_s)

    for sem, kept in ((m_s, y_hi == 0), (t_s, core == 0), (d_s, own)):
        @pl.when(kept)
        def _(sem=sem):
            wait(DP.at[0, 0, 0:7], sem)

        @pl.when(jnp.logical_not(kept))
        def _(sem=sem):
            wait(eight, sem)


def body(hidden, head_weight, vocab_head, targets):
    feats, units = head_weight.shape
    voc = vocab_head.shape[1]
    vq = voc // PARTS
    pairs = ROUNDS // 2
    dma = pltpu.SemaphoreType.DMA
    one = pltpu.SemaphoreType.DMA
    vmem = pltpu.VMEM
    scratch = [
        vmem((2 * ROUNDS, 128, feats), BF16),
        vmem((feats, units), BF16),
        vmem((units, voc), BF16),
        vmem((ROUNDS, 2, RING, 16, units), F32),
        vmem((2, ROUNDS, 16, units), BF16),
        vmem((2, ROUNDS, 4, 2, 16, units), BF16),
        vmem((pairs, 16, units), BF16),
        vmem((pairs, 16, units), F32),
        vmem((pairs, 16, units), BF16),
        vmem((pairs, RING, 16, units), BF16),
        vmem((pairs, RING, 16, units), BF16),
        vmem((ROUNDS, 16, units), BF16),
        vmem((ROUNDS, 16, units), BF16),
        vmem((8, 16, units), BF16),
        vmem((128, units), BF16),
        vmem((128, units), F32),
        vmem((PARTS, RING, 16, vq), F32),
        vmem((2, PARTS, 16, vq // 2), BF16),
        vmem((2, PARTS, 4, 16, vq), BF16),
        vmem((PARTS, 16, vq), BF16),
        vmem((PARTS, 16, vq), BF16),
        vmem((PARTS, 16, vq), F32),
        vmem((PARTS, RING, 16, vq), BF16),
        vmem((RING, 16, 128), BF16),
        vmem((128, units), F32),
        vmem((8, 16, units), BF16),
        vmem((ROUNDS, 2, RING, 16, units), BF16),
        vmem((units, feats), F32),
        dma((3,)),
        one, dma((2 * ROUNDS,)),
        dma((4,)), dma((2, ROUNDS, 4)),
        dma((2,)), dma((pairs,)), dma((pairs, 5)),
        one, dma((ROUNDS,)),
        one, one,
        dma((2,)), dma((2, PARTS, 4)),
        one, dma((PARTS,)),
        dma((2,)), dma((2, PARTS, 4)),
        one, dma((2, 4)),
        one, dma((ROUNDS,)),
        dma((2,)), dma((ROUNDS,)),
        dma((4,)), dma((2, ROUNDS, 4)),
    ]
    anywhere = pl.BlockSpec(memory_space=pl.ANY)
    inside = pl.BlockSpec(memory_space=pltpu.VMEM)
    grad, loss = pl.pallas_call(
        kernel,
        out_shape=[
            pltpu.VMEM((units, feats), BF16),
            jax.ShapeDtypeStruct((1, 128), F32),
        ],
        in_specs=[anywhere, anywhere, anywhere, inside],
        out_specs=[inside, inside],
        scratch_shapes=scratch,
        compiler_params=pltpu.CompilerParams(
            collective_id=0, has_side_effects=True, vmem_limit_bytes=56 * 1024 * 1024
        ),
        name="head",
    )(hidden, head_weight, vocab_head, targets.reshape(1, 128))
    return grad, loss.reshape(targets.shape)


def solution(mesh):
    in_specs = (P("dp", "shard"), P("shard", "dp"), P("shard", None), P("dp"))
    out_specs = (P("dp", "shard"), P("dp"))
    return jax.shard_map(body, mesh=mesh, in_specs=in_specs, out_specs=out_specs, check_vma=False)
```
